32 devices in a mesh: gx: 8 (over z, y), gy: 4 (over x, core).
Axes of the slice: x: 2, y: 2, z: 4, core: 2. Of those that a mesh axis runs over, the one named last changes fastest.
Arguments:
- rhs_field: float32 [3, 32, 32, 2048], P(None, None, 'gy', 'gx'), may hold values from -6 to 6
- couplings: float32 [6, 3, 3, 32, 32, 2048], P(None, None, None, None, 'gy', 'gx'), may hold values from -0.6 to 0.6
- pivot_inverses: float32 [3, 3, 32, 32, 2048], P(None, None, None, 'gy', 'gx'), may hold values from -3.5 to 3.5
- colours: int32 [32, 32, 2048], P(None, 'gy', 'gx'), may hold values from 0 to 3
- perf_cells: int32 [32768], P(('gx', 'gy')), may hold values from 0 to 65535
- perf_wells: int32 [32768], P(('gx', 'gy')), may hold values from 0 to 2047, as said below
- perf_segments: int32 [32768], P(('gx', 'gy')), may hold values from 0 to 15
- perf_gather: float32 [3, 32768], P(None, ('gx', 'gy')), may hold values from -3 to 3
- perf_return: float32 [3, 32768], P(None, ('gx', 'gy')), may hold values from -3 to 3
- well_slot: int32 [2048], replicated, may hold values from 0 to 2047, as said below
- seg_count: int32 [2048], replicated, may hold values from 1 to 16
- well_inverses: float32 [2048, 16, 16], P(('gx', 'gy')), may hold values from -1.5 to 1.5
Outputs:
- precond_field: float32 [3, 32, 32, 2048], P(None, None, 'gy', 'gx')
The draws below stay inside these ranges and needn't reach their ends.
Inputs may be any that keep to these rules, and one draw needn't show every extreme that they name: `well_slot`: wells are numbered by owner: well w's slot lies in w // 64 * 64 to that plus 64 - 1, each slot taken once, so slot s belongs to tile s // 64 (tiles ordered with x slowest). `perf_wells`: A perforation listed with a tile may name a well of any owner.
All inputs are finite; a program needn't handle non-finite values.
Results may differ from the reference program's by a relative error of at most 0.0001.
Values sent between devices are 32-bit elements; how exact they have to be, the bound alone decides.
A program may use at most 384 MiB of HBM per device.

```python
import jax
import jax.numpy as jnp
from jax import lax

CX = 256
CY = 8
NZ = 32
SEG = 16
WELL_DEV = 64
PERF_DEV = 1024
NX = 2048
NY = 32
CELLS_DEV = 65536
PERFS = 32768
WELLS = 2048
N_GY = 4
DEVICES = 32


def draw_perf_wells(key, part):
    index = jnp.arange(PERFS, dtype=jnp.int32)
    tile = index // PERF_DEV
    within = index % PERF_DEV
    owner_far = (tile + DEVICES // 2) % DEVICES
    owner_before = (tile + DEVICES - 1) % DEVICES
    owner_any = jax.random.randint(jax.random.fold_in(key, 11), (PERFS,), 0, DEVICES, dtype=jnp.int32)
    owner = jnp.where(within == 0, owner_far, jnp.where(within == 1, owner_before, owner_any))
    first = jax.random.randint(jax.random.fold_in(key, 12), (PERFS,), 0, WELL_DEV, dtype=jnp.int32)
    second = jax.random.randint(jax.random.fold_in(key, 13), (PERFS,), 0, WELL_DEV, dtype=jnp.int32)
    local_well = jnp.minimum(first, second)
    return (owner * WELL_DEV + local_well).astype(jnp.int32)


def draw_well_slot(key, part):
    blocks = jnp.arange(DEVICES, dtype=jnp.int32)

    def one_block(block):
        order = jax.random.permutation(jax.random.fold_in(jax.random.fold_in(key, 21), block), WELL_DEV)
        return (block * WELL_DEV + order).astype(jnp.int32)
    return jax.vmap(one_block)(blocks).reshape(-1).astype(jnp.int32)


def touch_ends(drawn, stream_key, smallest, high):
    longest = drawn.shape.index(max(drawn.shape))
    spots = []
    for shift in (0, 1):
        where = [jax.random.randint(jax.random.fold_in(stream_key, axis), (), 0, length) for axis, length in enumerate(drawn.shape)]
        where[longest] = (where[longest] + shift) % drawn.shape[longest]
        spots.append(tuple(where))
    return drawn.at[spots[0]].set(smallest).at[spots[1]].set(high)


def steps_of(stream_key, extent, split, least, top_value):
    def one(position, parts):
        heights = jax.random.uniform(jax.random.fold_in(jax.random.fold_in(stream_key, 6), position), (parts,), jnp.float32, least / len(split), top_value / len(split))
        return jnp.repeat(jnp.exp(heights), extent[position] // parts).reshape((-1,) + (1,) * (len(extent) - position - 1))

    gain = one(*split[0])
    for cut in split[1:]:
        gain = gain * one(*cut)
    return gain


def gaussian(stream_key, extent, deviation, most, split=(), kind=jnp.bfloat16):
    gain = steps_of(stream_key, extent, split, -0.22, 0.18) if split else 1.0
    result = jax.random.normal(stream_key, extent, jnp.float32) * deviation * gain
    return jnp.minimum(jnp.maximum(result, -most), most).astype(kind)


def setup_inputs(seed: int = 0) -> dict:
    arg_keys = jax.random.split(jax.random.key(seed), 13)
    rhs_field = gaussian(arg_keys[0], (3, NZ, NY, NX), 1.0, 6.0, ((2, 4), (3, 8)), jnp.float32)
    couplings = gaussian(arg_keys[1], (6, 3, 3, NZ, NY, NX), 0.12, 0.6, ((4, 4), (5, 8)), jnp.float32)
    pivot_inverses = gaussian(arg_keys[2], (3, 3, NZ, NY, NX), 3 ** -0.5, 3.5, ((3, 4), (4, 8)), jnp.float32)
    colours = touch_ends(jax.random.randint(arg_keys[3], (NZ, NY, NX), 0, 4), jax.random.fold_in(arg_keys[3], 1), 0, 3).astype(jnp.int32)
    perf_cells = touch_ends(jax.random.randint(arg_keys[4], (PERFS,), 0, CELLS_DEV), jax.random.fold_in(arg_keys[4], 1), 0, CELLS_DEV - 1).astype(jnp.int32)
    perf_wells = draw_perf_wells(jax.random.fold_in(arg_keys[12], 71), 0)
    perf_segments = touch_ends(jax.random.randint(arg_keys[6], (PERFS,), 0, SEG), jax.random.fold_in(arg_keys[6], 1), 0, SEG - 1).astype(jnp.int32)
    perf_gather = gaussian(arg_keys[7], (3, PERFS), 0.5, 3.0, ((1, 32),), jnp.float32)
    perf_return = gaussian(arg_keys[8], (3, PERFS), 0.5, 3.0, ((1, 32),), jnp.float32)
    well_slot = draw_well_slot(jax.random.fold_in(arg_keys[12], 71), 0)
    seg_count = touch_ends(jax.random.randint(arg_keys[10], (WELLS,), 1, SEG + 1), jax.random.fold_in(arg_keys[10], 1), 1, SEG).astype(jnp.int32)
    well_inverses = gaussian(arg_keys[11], (WELLS, SEG, SEG), SEG ** -0.5, 1.5, ((0, 32),), jnp.float32)
    return {"rhs_field": rhs_field, "couplings": couplings, "pivot_inverses": pivot_inverses, "colours": colours, "perf_cells": perf_cells, "perf_wells": perf_wells, "perf_segments": perf_segments, "perf_gather": perf_gather, "perf_return": perf_return, "well_slot": well_slot, "seg_count": seg_count, "well_inverses": well_inverses}


def couple(couplings, field):
    padded = jnp.pad(field, ((0, 0), (1, 1), (1, 1), (1, 1)))
    beside = jnp.stack([padded[:, 1:-1, 1:-1, :-2], padded[:, 1:-1, 1:-1, 2:], padded[:, 1:-1, :-2, 1:-1], padded[:, 1:-1, 2:, 1:-1], padded[:, :-2, 1:-1, 1:-1], padded[:, 2:, 1:-1, 1:-1]])
    return jnp.sum(couplings * beside[:, None], axis=(0, 2))


def pivot(pivot_inverses, field):
    return jnp.sum(pivot_inverses * field[None], axis=1)


def well_solve(inverses, totals, seg_counts):
    seg_index = jnp.arange(totals.shape[1], dtype=jnp.int32)
    alive_mask = (seg_index[None, :] < seg_counts[:, None]).astype(jnp.float32)
    return alive_mask * jnp.einsum("wst,wt->ws", inverses, alive_mask * totals, precision=lax.Precision.HIGHEST)


def reference(rhs_field, couplings, pivot_inverses, colours, perf_cells, perf_wells, perf_segments, perf_gather, perf_return, well_slot, seg_count, well_inverses):
    lower = jnp.zeros_like(rhs_field)
    upper_in = jnp.zeros_like(rhs_field)
    for colour in range(4):
        chosen = (colours == colour)[None]
        if colour == 0:
            current = rhs_field
        else:
            current = rhs_field - couple(couplings, lower)
        upper_in = jnp.where(chosen, current, upper_in)
        lower = jnp.where(chosen, pivot(pivot_inverses, current), lower)
    sweep_field = jnp.zeros_like(rhs_field)
    for colour in (3, 2, 1, 0):
        chosen = (colours == colour)[None]
        if colour == 3:
            current = pivot(pivot_inverses, upper_in)
        else:
            current = pivot(pivot_inverses, upper_in - couple(couplings, sweep_field))
        sweep_field = jnp.where(chosen, current, sweep_field)
    device = (jnp.arange(PERFS, dtype=jnp.int32) // PERF_DEV).astype(jnp.int32)
    tile_x = device // N_GY
    tile_y = device % N_GY
    layer = perf_cells // (CY * CX)
    row_y = tile_y * CY + (perf_cells // CX) % CY
    row_x = tile_x * CX + perf_cells % CX
    at_cells = sweep_field[:, layer, row_y, row_x]
    terms = jnp.sum(perf_gather * at_cells, axis=0)
    well_key = (well_slot[perf_wells] * SEG + perf_segments).astype(jnp.int32)
    totals = jnp.zeros((WELLS * SEG,), jnp.float32).at[well_key].add(terms).reshape(WELLS, SEG)
    slot_counts = jnp.zeros((WELLS,), jnp.int32).at[well_slot].set(seg_count)
    segment_values = well_solve(well_inverses, totals, slot_counts)
    at_perfs = segment_values.reshape(-1)[well_key]
    return sweep_field.at[:, layer, row_y, row_x].add(-perf_return * at_perfs[None])
```

```python
import functools

import jax
import jax.numpy as jnp
from jax import lax
from jax.experimental import pallas as pl
from jax.experimental.pallas import tpu as pltpu
from jax.sharding import PartitionSpec as P

MESH = pl.DeviceIdType.MESH
LANES = 128
F32 = jnp.float32
BF16 = jnp.bfloat16


def shift_of(n):
    assert n & (n - 1) == 0
    return n.bit_length() - 1


def parts_of(x, count=3):
    parts = []
    for k in range(count):
        part = x.astype(BF16)
        parts.append(part)
        if k + 1 < count:
            x = x - part.astype(F32)
    return parts


def dot_nn(a, b):
    return lax.dot_general(a, b, (((1,), (0,)), ((), ())), preferred_element_type=F32)


def dot_nt(a, b):
    return lax.dot_general(a, b, (((1,), (1,)), ((), ())), preferred_element_type=F32)


def dot_exact(a, b):
    return lax.dot_general(
        a, b, (((1,), (0,)), ((), ())), precision=lax.Precision.HIGHEST, preferred_element_type=F32
    )


def one_hot(row, count):
    index = lax.broadcasted_iota(jnp.int32, (count, row.shape[1]), 0)
    return jnp.where(index == row, 1.0, 0.0).astype(BF16)


def kernel(
    gx,
    gy,
    rhs,
    couplings,
    pivots,
    colours,
    cells,
    wells,
    segs,
    gather,
    ret,
    slots,
    counts,
    inverses,
    out,
    coup,
    fld,
    upper,
    acc,
    cx_edge,
    cy_edge,
    x_add,
    y_add,
    xsend,
    ysend,
    xhalo,
    yhalo,
    hot_x,
    hot_r,
    hot_hi,
    hot_lo,
    totals,
    got_a,
    sum_a,
    got_b,
    values,
    load_sem,
    halo_send,
    halo_recv,
    a_send,
    a_recv,
    b_send,
    b_recv,
    c_send,
    c_recv,
    d_send,
    d_recv,
):
    _, nz, cy, cx = rhs.shape
    owned, seg, _ = inverses.shape
    ix = lax.axis_index("gx")
    iy = lax.axis_index("gy")

    loads = [
        pltpu.make_async_copy(couplings.at[k], coup.at[k], load_sem.at[k]) for k in range(6)
    ]
    for load in loads:
        load.start()

    @pl.when(ix == 0)
    def _():
        xhalo[:, 0] = jnp.zeros_like(xhalo[:, 0])

    @pl.when(ix == gx - 1)
    def _():
        xhalo[:, 1] = jnp.zeros_like(xhalo[:, 1])

    @pl.when(iy == 0)
    def _():
        yhalo[:, 0] = jnp.zeros_like(yhalo[:, 0])

    @pl.when(iy == gy - 1)
    def _():
        yhalo[:, 1] = jnp.zeros_like(yhalo[:, 1])

    barrier = pltpu.get_barrier_semaphore()
    for d in range(1, gx):
        pl.semaphore_signal(
            barrier, inc=1, device_id=(lax.rem(ix + d, gx), iy), device_id_type=MESH
        )
    for d in range(1, gy):
        pl.semaphore_signal(
            barrier, inc=1, device_id=(ix, lax.rem(iy + d, gy)), device_id_type=MESH
        )

    lane = lax.broadcasted_iota(jnp.int32, (cy, LANES), 1)
    wide_lane = lax.broadcasted_iota(jnp.int32, (cy, cx), 1)
    row = lax.broadcasted_iota(jnp.int32, (cy, cx), 0)
    tiles = cx // LANES

    for u in range(3):
        fld[u, 0] = jnp.zeros((cy, cx), F32)
        fld[u, nz + 1] = jnp.zeros((cy, cx), F32)

    def pivoted(z, field):
        return [
            pivots[i, 0, z] * field[0] + pivots[i, 1, z] * field[1] + pivots[i, 2, z] * field[2]
            for i in range(3)
        ]

    def emit(slot, z, new, packs):
        result = []
        for j in range(3):
            ysend[slot, 0, j, pl.ds(z, 1), :] = new[j][cy - 1 : cy]
            ysend[slot, 1, j, pl.ds(z, 1), :] = new[j][0:1]
        for j in range(3):
            moved = pltpu.roll(new[j][:, cx - LANES :], z + 1, 1)
            result.append(jnp.where(lane == z, moved, packs[j]))
        for j in range(3):
            moved = pltpu.roll(new[j][:, :LANES], z, 1)
            result.append(jnp.where(lane == z, moved, packs[3 + j]))
        return tuple(result)

    no_packs = tuple(jnp.zeros((cy, LANES), F32) for _ in range(6))

    def halo_copies(slot):
        found = []
        for side, (buffers, there, inside) in enumerate(
            (
                ((xsend, xhalo), (ix + 1, iy), ix < gx - 1),
                ((xsend, xhalo), (ix - 1, iy), ix > 0),
                ((ysend, yhalo), (ix, iy + 1), iy < gy - 1),
                ((ysend, yhalo), (ix, iy - 1), iy > 0),
            )
        ):
            copy = pltpu.make_async_remote_copy(
                src_ref=buffers[0].at[slot, side % 2],
                dst_ref=buffers[1].at[slot, side % 2],
                send_sem=halo_send.at[slot, side],
                recv_sem=halo_recv.at[slot, side],
                device_id=there,
                device_id_type=MESH,
            )
            found.append((copy, inside))
        return found

    def send_halo(slot, packs):
        for j in range(3):
            xsend[slot, 0, j] = packs[j]
            xsend[slot, 1, j] = packs[3 + j]
        for copy, inside in halo_copies(slot):
            pl.when(inside)(copy.start)

    def take_halo(slot):
        copies = halo_copies(slot)
        for side in range(4):
            pl.when(copies[side ^ 1][1])(copies[side][0].wait_recv)
        for side in range(2):
            for i in range(3):
                x_add[side, i] = sum(cx_edge[side, i, j] * xhalo[slot, side, j] for j in range(3))
                y_add[side, i] = sum(cy_edge[side, i, j] * yhalo[slot, side, j] for j in range(3))

    def interior(base):
        def step(z, carry):
            total = [base[i, z] for i in range(3)]
            for j in range(3):
                here = fld[j, z + 1]
                beside = (
                    jnp.where(wide_lane == 0, 0.0, pltpu.roll(here, 1, 1)),
                    jnp.where(wide_lane == cx - 1, 0.0, pltpu.roll(here, cx - 1, 1)),
                    jnp.where(row == 0, 0.0, pltpu.roll(here, 1, 0)),
                    jnp.where(row == cy - 1, 0.0, pltpu.roll(here, cy - 1, 0)),
                    fld[j, z],
                    fld[j, z + 2],
                )
                for i in range(3):
                    for k in range(6):
                        total[i] = total[i] - coup[k, i, j, z] * beside[k]
            for i in range(3):
                acc[i, z] = total[i]
            return carry

        lax.fori_loop(0, nz, step, 0, unroll=2)

    def finish(colour, slot, forward):
        def step(z, packs):
            current = []
            for i in range(3):
                first = jnp.where(lane == 0, pltpu.roll(x_add[0, i], LANES - z, 1), 0.0)
                last = jnp.where(lane == LANES - 1, pltpu.roll(x_add[1, i], LANES - 1 - z, 1), 0.0)
                pieces = [jnp.zeros((cy, LANES), F32)] * tiles
                pieces[0] = pieces[0] + first
                pieces[-1] = pieces[-1] + last
                along_x = jnp.concatenate(pieces, axis=1) if tiles > 1 else pieces[0]
                along_y = jnp.where(row == 0, y_add[0, i, pl.ds(z, 1), :], 0.0) + jnp.where(
                    row == cy - 1, y_add[1, i, pl.ds(z, 1), :], 0.0
                )
                current.append(acc[i, z] - along_x - along_y)
            chosen = colours[z] == colour
            new = pivoted(z, current)
            for i in range(3):
                if forward:
                    upper[i, z] = jnp.where(chosen, current[i], upper[i, z])
                before = 0.0 if forward and colour == 3 else fld[i, z + 1]
                new[i] = jnp.where(chosen, new[i], before)
                fld[i, z + 1] = new[i]
            if slot is None:
                return packs
            return emit(slot, z, new, packs)

        packs = lax.fori_loop(0, nz, step, no_packs, unroll=2)
        if slot is not None:
            send_halo(slot, packs)

    def first(z, packs):
        chosen = colours[z] == 0
        field = [rhs[i, z] for i in range(3)]
        new = pivoted(z, field)
        for i in range(3):
            upper[i, z] = field[i]
            new[i] = jnp.where(chosen, new[i], 0.0)
            fld[i, z + 1] = new[i]
        return emit(0, z, new, packs)

    packs = lax.fori_loop(0, nz, first, no_packs, unroll=2)
    pl.semaphore_wait(barrier, gx + gy - 2)
    send_halo(0, packs)

    cell = cells[...]
    hot_x[...] = one_hot(cell & (cx - 1), cx)
    hot_r[...] = one_hot(cell >> shift_of(cx), nz * cy)
    per_owner = owned * seg // LANES
    key = wells[...] * seg + segs[...]
    high = key >> shift_of(LANES)
    owner = high >> shift_of(per_owner)
    placed = (owner & (gy - 1)) * gx + (owner >> shift_of(gy))
    high = placed * per_owner + (high & (per_owner - 1))
    hot_hi[...] = one_hot(high, gx * gy * per_owner)
    hot_lo[...] = one_hot(key & (LANES - 1), LANES)

    for load in loads:
        load.wait()

    for i in range(3):
        for j in range(3):

            def pack(z, carry):
                left, right = carry
                moved = pltpu.roll(coup[0, i, j, z][:, :LANES], z, 1)
                left = jnp.where(lane == z, moved, left)
                moved = pltpu.roll(coup[1, i, j, z][:, cx - LANES :], z + 1, 1)
                right = jnp.where(lane == z, moved, right)
                cy_edge[0, i, j, pl.ds(z, 1), :] = coup[2, i, j, z, 0:1, :]
                cy_edge[1, i, j, pl.ds(z, 1), :] = coup[3, i, j, z, cy - 1 : cy, :]
                return left, right

            left, right = lax.fori_loop(0, nz, pack, no_packs[:2], unroll=4)
            cx_edge[0, i, j] = left
            cx_edge[1, i, j] = right

    slot = 0
    for colour in (1, 2, 3):
        interior(rhs)
        take_halo(slot)
        slot += 1
        finish(colour, slot, True)
    for colour in (2, 1, 0):
        interior(upper)
        take_halo(slot)
        slot += 1
        finish(colour, slot if colour > 0 else None, False)

    term = jnp.zeros(hot_r.shape, F32)
    for u in range(3):
        field = fld[u, 1 : nz + 1].reshape(nz * cy, cx)
        read = sum(dot_nn(part, hot_x[...]) for part in parts_of(field))
        term = term + read * gather[u : u + 1, :]
    term = jnp.sum(term * hot_r[...].astype(F32), axis=0, keepdims=True)
    spread = hot_lo[...].astype(F32) * term
    sums = sum(dot_nt(hot_hi[...], part) for part in parts_of(spread))
    totals[...] = sums.reshape(totals.shape)

    def along_gy(src, dst, send, recv, d):
        return pltpu.make_async_remote_copy(
            src_ref=src,
            dst_ref=dst,
            send_sem=send.at[d],
            recv_sem=recv.at[d],
            device_id=(ix, lax.rem(iy + d, gy)),
            device_id_type=MESH,
        )

    def along_gx(src, dst, send, recv, d):
        return pltpu.make_async_remote_copy(
            src_ref=src,
            dst_ref=dst,
            send_sem=send.at[d],
            recv_sem=recv.at[d],
            device_id=(lax.rem(ix + d, gx), iy),
            device_id_type=MESH,
        )

    copies_a = [
        along_gy(totals.at[lax.rem(iy + d, gy)], got_a.at[d], a_send, a_recv, d)
        for d in range(1, gy)
    ]
    for copy in copies_a:
        copy.start()

    first_well = (ix * gy + iy) * owned
    at_row = lax.div(first_well, LANES)
    at_lane = lax.rem(first_well, LANES)

    def own_row(table):
        line = jnp.broadcast_to(table[pl.ds(at_row, 1), :], (8, LANES))
        return pltpu.roll(line, LANES - at_lane, 1)[0:1, :owned]

    slot_row = own_row(slots) - first_well
    count_row = own_row(counts)
    by_slot = lax.broadcasted_iota(jnp.int32, (owned, owned), 0)
    by_well = lax.broadcasted_iota(jnp.int32, (owned, owned), 1)
    order = jnp.where(slot_row == by_slot, 1.0, 0.0)
    live = jnp.sum(jnp.where(slot_row == by_slot, count_row, 0), axis=1, keepdims=True)
    slot_column = jnp.sum(jnp.where(by_slot == by_well, slot_row, 0), axis=1, keepdims=True)
    back_index = lax.broadcasted_iota(jnp.int32, (owned, owned * seg), 1) >> shift_of(seg)
    back = jnp.where(back_index == slot_column, 1.0, 0.0)
    wells_row = LANES // seg
    lane_of = lax.broadcasted_iota(jnp.int32, (owned, LANES), 1)
    well_of = lax.broadcasted_iota(jnp.int32, (owned, LANES), 0)
    mine = (lane_of >> shift_of(seg)) == (well_of & (wells_row - 1))
    fold_from = lax.broadcasted_iota(jnp.int32, (LANES, seg), 0)
    fold_to = lax.broadcasted_iota(jnp.int32, (LANES, seg), 1)
    fold = jnp.where((fold_from & (seg - 1)) == fold_to, 1.0, 0.0)
    segment = lax.broadcasted_iota(jnp.int32, (owned, seg), 1)

    for copy in copies_a:
        copy.wait_recv()
    summed = totals[iy]
    for d in range(1, gy):
        summed = summed + got_a[d]
    sum_a[...] = summed
    copies_b = [
        along_gx(sum_a.at[lax.rem(ix + d, gx)], got_b.at[d], b_send, b_recv, d)
        for d in range(1, gx)
    ]
    for copy in copies_b:
        copy.start()
    for copy in copies_b:
        copy.wait_recv()
    own = sum_a[ix]
    for d in range(1, gx):
        own = own + got_b[d]

    rows = jnp.broadcast_to(own[:, None, :], (per_owner, wells_row, LANES)).reshape(owned, LANES)
    by_segment = dot_exact(dot_exact(order, jnp.where(mine, rows, 0.0)), fold)
    by_segment = jnp.where(segment < live, by_segment, 0.0)
    solved = jnp.sum(inverses[...] * by_segment[:, None, :], axis=2, keepdims=True)
    inner = lax.broadcasted_iota(jnp.int32, (owned, seg, LANES), 1)
    outer = lax.broadcasted_iota(jnp.int32, (owned, seg, LANES), 2) & (seg - 1)
    alive = (inner == outer) & (inner < live[:, :, None])
    solved = jnp.where(alive, solved, 0.0).reshape(owned * seg, LANES)
    spread_back = jnp.where(mine, dot_exact(back, solved), 0.0)
    values[iy, ix] = jnp.sum(spread_back.reshape(per_owner, wells_row, LANES), axis=1)

    def sent_c(d):
        return along_gx(values.at[iy, ix], values.at[iy, ix], c_send, c_recv, d)

    def due_c(d):
        there = lax.rem(ix + gx - d, gx)
        return along_gx(values.at[iy, there], values.at[iy, there], c_send, c_recv, d)

    for d in range(1, gx):
        sent_c(d).start()
    for d in range(1, gx):
        due_c(d).wait_recv()

    def sent_d(d):
        return along_gy(values.at[iy], values.at[iy], d_send, d_recv, d)

    def due_d(d):
        there = lax.rem(iy + gy - d, gy)
        return along_gy(values.at[there], values.at[there], d_send, d_recv, d)

    for d in range(1, gy):
        sent_d(d).start()
    for d in range(1, gy):
        due_d(d).wait_recv()

    table = values[...].reshape(gx * gy * per_owner, LANES)
    read = sum(dot_nn(part, hot_lo[...]) for part in parts_of(table))
    at_perfs = jnp.sum(read * hot_hi[...].astype(F32), axis=0, keepdims=True)
    for u in range(3):
        weights = hot_x[...].astype(F32) * (ret[u : u + 1, :] * at_perfs)
        change = sum(dot_nt(hot_r[...], part) for part in parts_of(weights))
        out[u] = fld[u, 1 : nz + 1] - change.reshape(nz, cy, cx)

    for done in range(slot):
        for copy, inside in halo_copies(done):
            pl.when(inside)(copy.wait_send)
    for copy in copies_a + copies_b:
        copy.wait_send()
    for d in range(1, gx):
        sent_c(d).wait_send()
    for d in range(1, gy):
        sent_d(d).wait_send()


def shards(
    gx,
    gy,
    rhs_field,
    couplings,
    pivot_inverses,
    colours,
    perf_cells,
    perf_wells,
    perf_segments,
    perf_gather,
    perf_return,
    well_slot,
    seg_count,
    well_inverses,
):
    _, nz, cy, cx = rhs_field.shape
    owned, seg, _ = well_inverses.shape
    perfs = perf_cells.shape[0]
    per_owner = owned * seg // LANES
    high = gx * gy * per_owner
    vmem = pl.BlockSpec(memory_space=pltpu.VMEM)
    dma = pltpu.SemaphoreType.DMA
    return pl.pallas_call(
        functools.partial(kernel, gx, gy),
        out_shape=jax.ShapeDtypeStruct(rhs_field.shape, F32),
        in_specs=[vmem, pl.BlockSpec(memory_space=pl.ANY)] + [vmem] * 10,
        out_specs=vmem,
        scratch_shapes=[
            pltpu.VMEM(couplings.shape, F32),
            pltpu.VMEM((3, nz + 2, cy, cx), F32),
            pltpu.VMEM((3, nz, cy, cx), F32),
            pltpu.VMEM((3, nz, cy, cx), F32),
            pltpu.VMEM((2, 3, 3, cy, LANES), F32),
            pltpu.VMEM((2, 3, 3, nz, cx), F32),
            pltpu.VMEM((2, 3, cy, LANES), F32),
            pltpu.VMEM((2, 3, nz, cx), F32),
            pltpu.VMEM((6, 2, 3, cy, LANES), F32),
            pltpu.VMEM((6, 2, 3, nz, cx), F32),
            pltpu.VMEM((6, 2, 3, cy, LANES), F32),
            pltpu.VMEM((6, 2, 3, nz, cx), F32),
            pltpu.VMEM((cx, perfs), BF16),
            pltpu.VMEM((nz * cy, perfs), BF16),
            pltpu.VMEM((high, perfs), BF16),
            pltpu.VMEM((LANES, perfs), BF16),
            pltpu.VMEM((gy, gx, per_owner, LANES), F32),
            pltpu.VMEM((gy, gx, per_owner, LANES), F32),
            pltpu.VMEM((gx, per_owner, LANES), F32),
            pltpu.VMEM((gx, per_owner, LANES), F32),
            pltpu.VMEM((gy, gx, per_owner, LANES), F32),
            dma((6,)),
            dma((6, 4)),
            dma((6, 4)),
            dma((gy,)),
            dma((gy,)),
            dma((gx,)),
            dma((gx,)),
            dma((gx,)),
            dma((gx,)),
            dma((gy,)),
            dma((gy,)),
        ],
        compiler_params=pltpu.CompilerParams(
            collective_id=0, has_side_effects=True, vmem_limit_bytes=52 * 2**20
        ),
        name="precondition",
    )(
        rhs_field,
        couplings,
        pivot_inverses,
        colours,
        perf_cells.reshape(1, perfs),
        perf_wells.reshape(1, perfs),
        perf_segments.reshape(1, perfs),
        perf_gather,
        perf_return,
        well_slot.reshape(-1, LANES),
        seg_count.reshape(-1, LANES),
        well_inverses,
    )


def solution(mesh):
    return jax.shard_map(
        functools.partial(shards, mesh.shape["gx"], mesh.shape["gy"]),
        mesh=mesh,
        in_specs=(
            P(None, None, "gy", "gx"),
            P(None, None, None, None, "gy", "gx"),
            P(None, None, None, "gy", "gx"),
            P(None, "gy", "gx"),
            P(("gx", "gy")),
            P(("gx", "gy")),
            P(("gx", "gy")),
            P(None, ("gx", "gy")),
            P(None, ("gx", "gy")),
            P(),
            P(),
            P(("gx", "gy"), None, None),
        ),
        out_specs=P(None, None, "gy", "gx"),
        check_vma=False,
    )
```

```python
import functools

import jax
import jax.numpy as jnp
from jax import lax
from jax.experimental import pallas as pl
from jax.experimental.pallas import tpu as pltpu
from jax.sharding import PartitionSpec as P

MESH = pl.DeviceIdType.MESH
LANES = 128
F32 = jnp.float32
BF16 = jnp.bfloat16


def shift_of(n):
    assert n & (n - 1) == 0
    return n.bit_length() - 1


def parts_of(x, count=3):
    parts = []
    for k in range(count):
        part = x.astype(BF16)
        parts.append(part)
        if k + 1 < count:
            x = x - part.astype(F32)
    return parts


def dot_nn(a, b):
    return lax.dot_general(a, b, (((1,), (0,)), ((), ())), preferred_element_type=F32)


def dot_nt(a, b):
    return lax.dot_general(a, b, (((1,), (1,)), ((), ())), preferred_element_type=F32)


def one_hot(row, count):
    index = lax.broadcasted_iota(jnp.int32, (count, row.shape[1]), 0)
    return jnp.where(index == row, 1.0, 0.0).astype(BF16)


def kernel(
    gx,
    gy,
    rhs,
    couplings,
    pivots_in,
    colours_in,
    cells_in,
    wells_in,
    segs_in,
    gather_in,
    ret_in,
    slots_in,
    counts_in,
    inverses_in,
    out,
    upper,
    coup,
    pivots,
    colours,
    cells,
    wells,
    segs,
    gather,
    ret,
    slots,
    counts,
    inverses,
    fld,
    acc,
    cx_edge,
    cy_edge,
    x_add,
    y_add,
    xsend,
    ysend,
    xhalo,
    yhalo,
    hot_x,
    hot_r,
    hot_hi,
    hot_lo,
    field_parts,
    terms,
    totals,
    got_a,
    sum_a,
    got_b,
    values,
    load_sem,
    small_sem,
    halo_send,
    halo_recv,
    a_send,
    a_recv,
    b_send,
    b_recv,
    c_send,
    c_recv,
    d_send,
    d_recv,
):
    _, nz, cy, cx = rhs.shape
    seg, _, owned = inverses.shape
    perfs = cells.shape[1]
    ix = lax.axis_index("gx")
    iy = lax.axis_index("gy")

    smalls = [
        pltpu.make_async_copy(src, dst, small_sem.at[k])
        for k, (src, dst) in enumerate(
            (
                (rhs, upper),
                (pivots_in, pivots),
                (colours_in, colours),
                (cells_in, cells),
                (wells_in, wells),
                (segs_in, segs),
                (gather_in, gather),
                (ret_in, ret),
                (slots_in, slots),
                (counts_in, counts),
                (inverses_in, inverses),
            )
        )
    ]
    loads = [
        pltpu.make_async_copy(couplings.at[k], coup.at[k], load_sem.at[k]) for k in range(6)
    ]
    for load in smalls + loads:
        load.start()

    barrier = pltpu.get_barrier_semaphore()

    @pl.when(ix == 0)
    def _():
        xhalo[:, 0] = jnp.zeros_like(xhalo[:, 0])

    @pl.when(ix == gx - 1)
    def _():
        xhalo[:, 1] = jnp.zeros_like(xhalo[:, 1])

    @pl.when(iy == 0)
    def _():
        yhalo[:, 0] = jnp.zeros_like(yhalo[:, 0])

    @pl.when(iy == gy - 1)
    def _():
        yhalo[:, 1] = jnp.zeros_like(yhalo[:, 1])

    for d in range(1, gx):
        pl.semaphore_signal(
            barrier, inc=1, device_id=(lax.rem(ix + d, gx), iy), device_id_type=MESH
        )
    for d in range(1, gy):
        pl.semaphore_signal(
            barrier, inc=1, device_id=(ix, lax.rem(iy + d, gy)), device_id_type=MESH
        )

    lane = lax.broadcasted_iota(jnp.int32, (cy, LANES), 1)
    wide_lane = lax.broadcasted_iota(jnp.int32, (cy, cx), 1)
    row = lax.broadcasted_iota(jnp.int32, (cy, cx), 0)
    tiles = cx // LANES

    for u in range(3):
        fld[u, 0] = jnp.zeros((cy, cx), F32)
        fld[u, nz + 1] = jnp.zeros((cy, cx), F32)

    def pivoted(z, field):
        return [
            pivots[i, 0, z] * field[0] + pivots[i, 1, z] * field[1] + pivots[i, 2, z] * field[2]
            for i in range(3)
        ]

    def emit(slot, z, new, packs):
        result = []
        for j in range(3):
            ysend[slot, 0, j, pl.ds(z, 1), :] = new[j][cy - 1 : cy]
            ysend[slot, 1, j, pl.ds(z, 1), :] = new[j][0:1]
        for j in range(3):
            moved = pltpu.roll(new[j][:, cx - LANES :], z + 1, 1)
            result.append(jnp.where(lane == z, moved, packs[j]))
        for j in range(3):
            moved = pltpu.roll(new[j][:, :LANES], z, 1)
            result.append(jnp.where(lane == z, moved, packs[3 + j]))
        return tuple(result)

    no_packs = tuple(jnp.zeros((cy, LANES), F32) for _ in range(6))

    def halo_copies(slot):
        found = []
        for side, (buffers, there, inside) in enumerate(
            (
                ((xsend, xhalo), (ix + 1, iy), ix < gx - 1),
                ((xsend, xhalo), (ix - 1, iy), ix > 0),
                ((ysend, yhalo), (ix, iy + 1), iy < gy - 1),
                ((ysend, yhalo), (ix, iy - 1), iy > 0),
            )
        ):
            copy = pltpu.make_async_remote_copy(
                src_ref=buffers[0].at[slot, side % 2],
                dst_ref=buffers[1].at[slot, side % 2],
                send_sem=halo_send.at[slot, side],
                recv_sem=halo_recv.at[slot, side],
                device_id=there,
                device_id_type=MESH,
            )
            found.append((copy, inside))
        return found

    def send_halo(slot, packs):
        for j in range(3):
            xsend[slot, 0, j] = packs[j]
            xsend[slot, 1, j] = packs[3 + j]
        for copy, inside in halo_copies(slot):
            pl.when(inside)(copy.start)

    def take_halo(slot):
        copies = halo_copies(slot)
        for side in range(4):
            pl.when(copies[side ^ 1][1])(copies[side][0].wait_recv)
        for side in range(2):
            for i in range(3):
                x_add[side, i] = sum(cx_edge[side, i, j] * xhalo[slot, side, j] for j in range(3))
                y_add[side, i] = sum(cy_edge[side, i, j] * yhalo[slot, side, j] for j in range(3))

    def interior(z, carry):
        total = [upper[i, z] for i in range(3)]
        for j in range(3):
            here = fld[j, z + 1]
            beside = (
                jnp.where(wide_lane == 0, 0.0, pltpu.roll(here, 1, 1)),
                jnp.where(wide_lane == cx - 1, 0.0, pltpu.roll(here, cx - 1, 1)),
                jnp.where(row == 0, 0.0, pltpu.roll(here, 1, 0)),
                jnp.where(row == cy - 1, 0.0, pltpu.roll(here, cy - 1, 0)),
                fld[j, z],
                fld[j, z + 2],
            )
            for i in range(3):
                for k in range(6):
                    total[i] = total[i] - coup[k, i, j, z] * beside[k]
        for i in range(3):
            acc[i, z] = total[i]
        return carry

    def finish(turn, colour, z, packs):
        current = []
        for i in range(3):
            first = jnp.where(lane == 0, pltpu.roll(x_add[0, i], LANES - z, 1), 0.0)
            last = jnp.where(lane == LANES - 1, pltpu.roll(x_add[1, i], LANES - 1 - z, 1), 0.0)
            pieces = [jnp.zeros((cy, LANES), F32)] * tiles
            pieces[0] = pieces[0] + first
            pieces[-1] = pieces[-1] + last
            along_x = jnp.concatenate(pieces, axis=1) if tiles > 1 else pieces[0]
            along_y = jnp.where(row == 0, y_add[0, i, pl.ds(z, 1), :], 0.0) + jnp.where(
                row == cy - 1, y_add[1, i, pl.ds(z, 1), :], 0.0
            )
            current.append(acc[i, z] - along_x - along_y)
        chosen = colours[z] == colour
        new = pivoted(z, current)
        kept = jnp.where(turn == 3, 0.0, 1.0)
        for i in range(3):
            upper[i, z] = jnp.where(chosen, current[i], upper[i, z])
            new[i] = jnp.where(chosen, new[i], fld[i, z + 1] * kept)
            fld[i, z + 1] = new[i]
        return emit(turn, z, new, packs)

    def first(z, packs):
        chosen = colours[z] == 0
        new = pivoted(z, [upper[i, z] for i in range(3)])
        for i in range(3):
            new[i] = jnp.where(chosen, new[i], 0.0)
            fld[i, z + 1] = new[i]
        return emit(0, z, new, packs)

    for load in smalls[:3]:
        load.wait()
    packs = lax.fori_loop(0, nz, first, no_packs, unroll=8)
    pl.semaphore_wait(barrier, gx + gy - 2)
    send_halo(0, packs)

    for load in smalls[3:]:
        load.wait()
    cell = cells[...]
    key = wells[...] * seg + segs[...]
    hot_x[...] = one_hot(cell & (cx - 1), cx)
    hot_r[...] = one_hot(cell >> shift_of(cx), nz * cy)
    per_owner = owned * seg // LANES
    high = key >> shift_of(LANES)
    owner = high >> shift_of(per_owner)
    placed = (owner & (gy - 1)) * gx + (owner >> shift_of(gy))
    high = placed * per_owner + (high & (per_owner - 1))
    hot_hi[...] = one_hot(high, gx * gy * per_owner)
    hot_lo[...] = one_hot(key & (LANES - 1), LANES)

    for load in loads:
        load.wait()

    def pack_edges(i, carry):
        for j in range(3):

            def pack(z, carry):
                left, right = carry
                moved = pltpu.roll(coup[0, i, j, z][:, :LANES], z, 1)
                left = jnp.where(lane == z, moved, left)
                moved = pltpu.roll(coup[1, i, j, z][:, cx - LANES :], z + 1, 1)
                right = jnp.where(lane == z, moved, right)
                cy_edge[0, i, j, pl.ds(z, 1), :] = coup[2, i, j, z, 0:1, :]
                cy_edge[1, i, j, pl.ds(z, 1), :] = coup[3, i, j, z, cy - 1 : cy, :]
                return left, right

            left, right = lax.fori_loop(0, nz, pack, no_packs[:2], unroll=16)
            cx_edge[0, i, j] = left
            cx_edge[1, i, j] = right
        return carry

    lax.fori_loop(0, 3, pack_edges, 0)

    def one_turn(turn, carry):
        colour = 3 - jnp.abs(turn - 3)
        lax.fori_loop(0, nz, interior, 0, unroll=4)
        take_halo(turn - 1)
        packs = lax.fori_loop(
            0, nz, functools.partial(finish, turn, colour), no_packs, unroll=8
        )

        @pl.when(turn < 6)
        def _():
            send_halo(turn, packs)

        return carry

    lax.fori_loop(1, 7, one_turn, 0)

    for u in range(3):
        for k, part in enumerate(parts_of(fld[u, 1 : nz + 1].reshape(nz * cy, cx), 2)):
            field_parts[u, k] = part
    chunk = min(perfs, 256)
    row_index = lax.broadcasted_iota(jnp.int32, (nz * cy, chunk), 0)

    def read_terms(c, carry):
        at = pl.ds(pl.multiple_of(c * chunk, chunk), chunk)
        column = hot_x[:, at]
        term = jnp.zeros((nz * cy, chunk), F32)
        for u in range(3):
            read = dot_nn(field_parts[u, 0], column) + dot_nn(field_parts[u, 1], column)
            term = term + read * gather[u : u + 1, at]
        there = cells[:, at] >> shift_of(cx)
        terms[:, at] = jnp.sum(jnp.where(row_index == there, term, 0.0), axis=0, keepdims=True)
        return carry

    lax.fori_loop(0, perfs // chunk, read_terms, 0)
    sums = sum(dot_nt(hot_hi[...], hot_lo[...] * part) for part in parts_of(terms[...]))
    totals[...] = sums.reshape(totals.shape)

    def along_gy(src, dst, send, recv, d):
        return pltpu.make_async_remote_copy(
            src_ref=src,
            dst_ref=dst,
            send_sem=send.at[d],
            recv_sem=recv.at[d],
            device_id=(ix, lax.rem(iy + d, gy)),
            device_id_type=MESH,
        )

    def along_gx(src, dst, send, recv, d):
        return pltpu.make_async_remote_copy(
            src_ref=src,
            dst_ref=dst,
            send_sem=send.at[d],
            recv_sem=recv.at[d],
            device_id=(lax.rem(ix + d, gx), iy),
            device_id_type=MESH,
        )

    copies_a = [
        along_gy(totals.at[lax.rem(iy + d, gy)], got_a.at[d], a_send, a_recv, d)
        for d in range(1, gy)
    ]
    for copy in copies_a:
        copy.start()

    first_well = (ix * gy + iy) * owned
    at_row = lax.div(first_well, LANES)
    at_lane = lax.rem(first_well, LANES)

    def own_row(table):
        line = jnp.broadcast_to(table[pl.ds(at_row, 1), :], (8, LANES))
        return pltpu.roll(line, LANES - at_lane, 1)[0:1, :owned]

    slot_row = own_row(slots) - first_well
    count_row = own_row(counts)
    down = lax.broadcasted_iota(jnp.int32, (owned, owned), 0)
    across = lax.broadcasted_iota(jnp.int32, (owned, owned), 1)
    slot_column = jnp.sum(jnp.where(down == across, slot_row, 0), axis=1, keepdims=True)
    count_column = jnp.sum(jnp.where(down == across, count_row, 0), axis=1, keepdims=True)
    to_slot = jnp.where(slot_row == down, 1.0, 0.0).astype(BF16)
    of_well = slot_column == across
    to_well = jnp.where(of_well, 1.0, 0.0).astype(BF16)
    live = jnp.sum(jnp.where(of_well, count_column, 0), axis=0, keepdims=True)
    alive = lax.broadcasted_iota(jnp.int32, (seg, owned), 0) < live
    wells_row = LANES // seg
    lane_of = lax.broadcasted_iota(jnp.int32, (owned, LANES), 1)
    well_of = lax.broadcasted_iota(jnp.int32, (owned, LANES), 0)
    mine = (lane_of >> shift_of(seg)) == (well_of & (wells_row - 1))
    fold_from = lax.broadcasted_iota(jnp.int32, (seg, LANES), 1)
    fold_to = lax.broadcasted_iota(jnp.int32, (seg, LANES), 0)
    fold = jnp.where((fold_from & (seg - 1)) == fold_to, 1.0, 0.0).astype(BF16)

    for copy in copies_a:
        copy.wait_recv()
    summed = totals[iy]
    for d in range(1, gy):
        summed = summed + got_a[d]
    sum_a[...] = summed
    copies_b = [
        along_gx(sum_a.at[lax.rem(ix + d, gx)], got_b.at[d], b_send, b_recv, d)
        for d in range(1, gx)
    ]
    for copy in copies_b:
        copy.start()
    for copy in copies_b:
        copy.wait_recv()
    own = sum_a[ix]
    for d in range(1, gx):
        own = own + got_b[d]

    rows = jnp.broadcast_to(own[:, None, :], (per_owner, wells_row, LANES)).reshape(owned, LANES)
    by_well = sum(dot_nt(fold, part) for part in parts_of(jnp.where(mine, rows, 0.0)))
    by_slot = sum(dot_nt(part, to_slot) for part in parts_of(by_well))
    by_slot = jnp.where(alive, by_slot, 0.0)
    solved = jnp.sum(inverses[...] * by_slot[None], axis=1)
    solved = jnp.where(alive, solved, 0.0)
    solved = sum(dot_nt(to_well, part) for part in parts_of(solved))
    solved = sum(dot_nn(part, fold) for part in parts_of(solved))
    solved = jnp.where(mine, solved, 0.0)
    values[iy, ix] = jnp.sum(solved.reshape(per_owner, wells_row, LANES), axis=1)

    def sent_c(d):
        return along_gx(values.at[iy, ix], values.at[iy, ix], c_send, c_recv, d)

    def due_c(d):
        there = lax.rem(ix + gx - d, gx)
        return along_gx(values.at[iy, there], values.at[iy, there], c_send, c_recv, d)

    for d in range(1, gx):
        sent_c(d).start()
    for d in range(1, gx):
        due_c(d).wait_recv()

    def sent_d(d):
        return along_gy(values.at[iy], values.at[iy], d_send, d_recv, d)

    def due_d(d):
        there = lax.rem(iy + gy - d, gy)
        return along_gy(values.at[there], values.at[there], d_send, d_recv, d)

    for d in range(1, gy):
        sent_d(d).start()
    for d in range(1, gy):
        due_d(d).wait_recv()

    table = values[...].reshape(gx * gy * per_owner, LANES)
    table_parts = parts_of(table)
    for c in range(perfs // chunk):
        at = pl.ds(c * chunk, chunk)
        column = hot_lo[:, at]
        read = sum(dot_nn(part, column) for part in table_parts)
        terms[:, at] = jnp.sum(read * hot_hi[:, at].astype(F32), axis=0, keepdims=True)
    at_perfs = terms[...]
    for u in range(3):
        weights = parts_of(ret[u : u + 1, :] * at_perfs, 2)
        change = sum(dot_nt(hot_r[...], hot_x[...] * part) for part in weights)
        out[u] = fld[u, 1 : nz + 1] - change.reshape(nz, cy, cx)

    for done in range(6):
        for copy, inside in halo_copies(done):
            pl.when(inside)(copy.wait_send)
    for copy in copies_a + copies_b:
        copy.wait_send()
    for d in range(1, gx):
        sent_c(d).wait_send()
    for d in range(1, gy):
        sent_d(d).wait_send()


def shards(
    gx,
    gy,
    rhs_field,
    couplings,
    pivot_inverses,
    colours,
    perf_cells,
    perf_wells,
    perf_segments,
    perf_gather,
    perf_return,
    well_slot,
    seg_count,
    well_inverses,
):
    _, nz, cy, cx = rhs_field.shape
    owned, seg, _ = well_inverses.shape
    perfs = perf_cells.shape[0]
    per_owner = owned * seg // LANES
    high = gx * gy * per_owner
    hbm = pl.BlockSpec(memory_space=pltpu.HBM)
    dma = pltpu.SemaphoreType.DMA
    operands = (
        rhs_field,
        couplings,
        pivot_inverses,
        colours,
        perf_cells.reshape(1, perfs),
        perf_wells.reshape(1, perfs),
        perf_segments.reshape(1, perfs),
        perf_gather,
        perf_return,
        well_slot.reshape(-1, LANES),
        seg_count.reshape(-1, LANES),
        jnp.transpose(well_inverses, (1, 2, 0)),
    )
    return pl.pallas_call(
        functools.partial(kernel, gx, gy),
        out_shape=jax.ShapeDtypeStruct(rhs_field.shape, F32),
        in_specs=[hbm] * len(operands),
        out_specs=pl.BlockSpec(memory_space=pltpu.VMEM),
        scratch_shapes=[pltpu.VMEM(x.shape, x.dtype) for x in operands]
        + [
            pltpu.VMEM((3, nz + 2, cy, cx), F32),
            pltpu.VMEM((3, nz, cy, cx), F32),
            pltpu.VMEM((2, 3, 3, cy, LANES), F32),
            pltpu.VMEM((2, 3, 3, nz, cx), F32),
            pltpu.VMEM((2, 3, cy, LANES), F32),
            pltpu.VMEM((2, 3, nz, cx), F32),
            pltpu.VMEM((6, 2, 3, cy, LANES), F32),
            pltpu.VMEM((7, 2, 3, nz, cx), F32),
            pltpu.VMEM((6, 2, 3, cy, LANES), F32),
            pltpu.VMEM((6, 2, 3, nz, cx), F32),
            pltpu.VMEM((cx, perfs), BF16),
            pltpu.VMEM((nz * cy, perfs), BF16),
            pltpu.VMEM((high, perfs), BF16),
            pltpu.VMEM((LANES, perfs), BF16),
            pltpu.VMEM((3, 2, nz * cy, cx), BF16),
            pltpu.VMEM((1, perfs), F32),
            pltpu.VMEM((gy, gx, per_owner, LANES), F32),
            pltpu.VMEM((gy, gx, per_owner, LANES), F32),
            pltpu.VMEM((gx, per_owner, LANES), F32),
            pltpu.VMEM((gx, per_owner, LANES), F32),
            pltpu.VMEM((gy, gx, per_owner, LANES), F32),
            dma((6,)),
            dma((11,)),
            dma((6, 4)),
            dma((6, 4)),
            dma((gy,)),
            dma((gy,)),
            dma((gx,)),
            dma((gx,)),
            dma((gx,)),
            dma((gx,)),
            dma((gy,)),
            dma((gy,)),
        ],
        compiler_params=pltpu.CompilerParams(
            collective_id=0, has_side_effects=True, vmem_limit_bytes=63 * 2**20 + 2**19
        ),
        name="precondition",
    )(*operands)


def solution(mesh):
    return jax.shard_map(
        functools.partial(shards, mesh.shape["gx"], mesh.shape["gy"]),
        mesh=mesh,
        in_specs=(
            P(None, None, "gy", "gx"),
            P(None, None, None, None, "gy", "gx"),
            P(None, None, None, "gy", "gx"),
            P(None, "gy", "gx"),
            P(("gx", "gy")),
            P(("gx", "gy")),
            P(("gx", "gy")),
            P(None, ("gx", "gy")),
            P(None, ("gx", "gy")),
            P(),
            P(),
            P(("gx", "gy"), None, None),
        ),
        out_specs=P(None, None, "gy", "gx"),
        check_vma=False,
    )
```

```python
import functools

import jax
import jax.numpy as jnp
from jax import lax
from jax.experimental import pallas as pl
from jax.experimental.pallas import tpu as pltpu
from jax.sharding import PartitionSpec as P

MESH = pl.DeviceIdType.MESH
LANES = 128
F32 = jnp.float32
BF16 = jnp.bfloat16


def shift_of(n):
    assert n & (n - 1) == 0
    return n.bit_length() - 1


def parts_of(x, count=3):
    parts = []
    for k in range(count):
        part = x.astype(BF16)
        parts.append(part)
        if k + 1 < count:
            x = x - part.astype(F32)
    return parts


def dot_nn(a, b):
    return lax.dot_general(a, b, (((1,), (0,)), ((), ())), preferred_element_type=F32)


def dot_nt(a, b):
    return lax.dot_general(a, b, (((1,), (1,)), ((), ())), preferred_element_type=F32)


def one_hot(row, count):
    index = lax.broadcasted_iota(jnp.int32, (count, row.shape[1]), 0)
    return jnp.where(index == row, 1.0, 0.0).astype(BF16)


def kernel(
    gx,
    gy,
    rhs,
    couplings,
    pivots_in,
    colours_in,
    cells_in,
    wells_in,
    segs_in,
    gather_in,
    ret_in,
    slots_in,
    counts_in,
    inverses_in,
    out,
    upper,
    coup,
    pivots,
    colours,
    cells,
    wells,
    segs,
    gather,
    ret,
    slots,
    counts,
    inverses,
    fld,
    acc,
    cx_edge,
    cy_edge,
    x_add,
    y_add,
    xsend,
    ysend,
    xhalo,
    yhalo,
    hot_x,
    hot_r,
    hot_hi,
    hot_lo,
    field_parts,
    terms,
    totals,
    got_a,
    sum_a,
    got_b,
    values,
    load_sem,
    small_sem,
    x_send,
    x_recv,
    y_send,
    y_recv,
    a_send,
    a_recv,
    b_send,
    b_recv,
    c_send,
    c_recv,
    d_send,
    d_recv,
):
    _, nz, cy, cx = rhs.shape
    seg, _, owned = inverses.shape
    perfs = cells.shape[1]
    depth = 8
    ix = lax.axis_index("gx")
    iy = lax.axis_index("gy")

    smalls = [
        pltpu.make_async_copy(src, dst, small_sem.at[k])
        for k, (src, dst) in enumerate(
            (
                (rhs, upper),
                (pivots_in, pivots),
                (colours_in, colours),
                (cells_in, cells),
                (wells_in, wells),
                (segs_in, segs),
                (gather_in, gather),
                (ret_in, ret),
                (slots_in, slots),
                (counts_in, counts),
                (inverses_in, inverses),
            )
        )
    ]
    loads = [
        pltpu.make_async_copy(couplings.at[k], coup.at[k], load_sem.at[k]) for k in range(6)
    ]
    for load in smalls + loads:
        load.start()

    barrier = pltpu.get_barrier_semaphore()

    @pl.when(ix == 0)
    def _():
        xhalo[:, 0] = jnp.zeros_like(xhalo[:, 0])

    @pl.when(ix == gx - 1)
    def _():
        xhalo[:, 1] = jnp.zeros_like(xhalo[:, 1])

    @pl.when(iy == 0)
    def _():
        yhalo[:, 0] = jnp.zeros_like(yhalo[:, 0])

    @pl.when(iy == gy - 1)
    def _():
        yhalo[:, 1] = jnp.zeros_like(yhalo[:, 1])

    for d in range(1, gx):
        pl.semaphore_signal(
            barrier, inc=1, device_id=(lax.rem(ix + d, gx), iy), device_id_type=MESH
        )
    for d in range(1, gy):
        pl.semaphore_signal(
            barrier, inc=1, device_id=(ix, lax.rem(iy + d, gy)), device_id_type=MESH
        )

    lane = lax.broadcasted_iota(jnp.int32, (cy, LANES), 1)
    wide_lane = lax.broadcasted_iota(jnp.int32, (cy, cx), 1)
    row = lax.broadcasted_iota(jnp.int32, (cy, cx), 0)
    tiles = cx // LANES

    for u in range(3):
        fld[u, 0] = jnp.zeros((cy, cx), F32)
        fld[u, nz + 1] = jnp.zeros((cy, cx), F32)

    def pivoted(z, field):
        return [
            pivots[i, 0, z] * field[0] + pivots[i, 1, z] * field[1] + pivots[i, 2, z] * field[2]
            for i in range(3)
        ]

    def emit(slot, z, new, packs):
        result = []
        for j in range(3):
            ysend[slot, 0, j, pl.ds(z, 1), :] = new[j][cy - 1 : cy]
            ysend[slot, 1, j, pl.ds(z, 1), :] = new[j][0:1]
        for j in range(3):
            moved = pltpu.roll(new[j][:, cx - LANES :], z + 1, 1)
            result.append(jnp.where(lane == z, moved, packs[j]))
        for j in range(3):
            moved = pltpu.roll(new[j][:, :LANES], z, 1)
            result.append(jnp.where(lane == z, moved, packs[3 + j]))
        return tuple(result)

    no_packs = tuple(jnp.zeros((cy, LANES), F32) for _ in range(6))

    def x_copies(slot):
        found = []
        for side, there, inside in ((0, ix + 1, ix < gx - 1), (1, ix - 1, ix > 0)):
            copy = pltpu.make_async_remote_copy(
                src_ref=xsend.at[slot, side],
                dst_ref=xhalo.at[slot, side],
                send_sem=x_send.at[slot, side],
                recv_sem=x_recv.at[slot, side],
                device_id=(there, iy),
                device_id_type=MESH,
            )
            found.append((copy, inside))
        return found

    def y_copies(slot, c):
        found = []
        layers = pl.ds(pl.multiple_of(c * depth, depth), depth)
        for side, there, inside in ((0, iy + 1, iy < gy - 1), (1, iy - 1, iy > 0)):
            copy = pltpu.make_async_remote_copy(
                src_ref=ysend.at[slot, side, :, layers, :],
                dst_ref=yhalo.at[slot, side, :, layers, :],
                send_sem=y_send.at[slot, c, side],
                recv_sem=y_recv.at[slot, c, side],
                device_id=(ix, there),
                device_id_type=MESH,
            )
            found.append((copy, inside))
        return found

    def sweep_layers(slot, body):
        def some(c, packs):
            for k in range(depth):
                packs = body(c * depth + k, packs)

            @pl.when(slot < 6)
            def _():
                for copy, inside in y_copies(slot, c):
                    pl.when(inside)(copy.start)

            return packs

        return lax.fori_loop(0, nz // depth, some, no_packs)

    def send_halo(slot, packs):
        for j in range(3):
            xsend[slot, 0, j] = packs[j]
            xsend[slot, 1, j] = packs[3 + j]
        for copy, inside in x_copies(slot):
            pl.when(inside)(copy.start)

    def take_halo(slot):
        copies = [x_copies(slot)] + [y_copies(slot, c) for c in range(nz // depth)]
        for pair in copies:
            pl.when(pair[1][1])(pair[0][0].wait_recv)
            pl.when(pair[0][1])(pair[1][0].wait_recv)
        for side in range(2):
            for i in range(3):
                x_add[side, i] = sum(cx_edge[side, i, j] * xhalo[slot, side, j] for j in range(3))
                y_add[side, i] = sum(cy_edge[side, i, j] * yhalo[slot, side, j] for j in range(3))

    def interior(z, carry):
        total = [upper[i, z] for i in range(3)]
        for j in range(3):
            here = fld[j, z + 1]
            beside = (
                jnp.where(wide_lane == 0, 0.0, pltpu.roll(here, 1, 1)),
                jnp.where(wide_lane == cx - 1, 0.0, pltpu.roll(here, cx - 1, 1)),
                jnp.where(row == 0, 0.0, pltpu.roll(here, 1, 0)),
                jnp.where(row == cy - 1, 0.0, pltpu.roll(here, cy - 1, 0)),
                fld[j, z],
                fld[j, z + 2],
            )
            for i in range(3):
                for k in range(6):
                    total[i] = total[i] - coup[k, i, j, z] * beside[k]
        for i in range(3):
            acc[i, z] = total[i]
        return carry

    def finish(turn, colour, z, packs):
        current = []
        for i in range(3):
            first = jnp.where(lane == 0, pltpu.roll(x_add[0, i], LANES - z, 1), 0.0)
            last = jnp.where(lane == LANES - 1, pltpu.roll(x_add[1, i], LANES - 1 - z, 1), 0.0)
            pieces = [jnp.zeros((cy, LANES), F32)] * tiles
            pieces[0] = pieces[0] + first
            pieces[-1] = pieces[-1] + last
            along_x = jnp.concatenate(pieces, axis=1) if tiles > 1 else pieces[0]
            along_y = jnp.where(row == 0, y_add[0, i, pl.ds(z, 1), :], 0.0) + jnp.where(
                row == cy - 1, y_add[1, i, pl.ds(z, 1), :], 0.0
            )
            current.append(acc[i, z] - along_x - along_y)
        chosen = colours[z] == colour
        new = pivoted(z, current)
        kept = jnp.where(turn == 3, 0.0, 1.0)
        for i in range(3):
            upper[i, z] = jnp.where(chosen, current[i], upper[i, z])
            new[i] = jnp.where(chosen, new[i], fld[i, z + 1] * kept)
            fld[i, z + 1] = new[i]
        return emit(turn, z, new, packs)

    def first(z, packs):
        chosen = colours[z] == 0
        new = pivoted(z, [upper[i, z] for i in range(3)])
        for i in range(3):
            new[i] = jnp.where(chosen, new[i], 0.0)
            fld[i, z + 1] = new[i]
        return emit(0, z, new, packs)

    for load in smalls[:3]:
        load.wait()
    pl.semaphore_wait(barrier, gx + gy - 2)
    packs = sweep_layers(0, first)
    send_halo(0, packs)

    for load in smalls[3:]:
        load.wait()
    cell = cells[...]
    key = wells[...] * seg + segs[...]
    hot_x[...] = one_hot(cell & (cx - 1), cx)
    hot_r[...] = one_hot(cell >> shift_of(cx), nz * cy)
    per_owner = owned * seg // LANES
    high = key >> shift_of(LANES)
    owner = high >> shift_of(per_owner)
    placed = (owner & (gy - 1)) * gx + (owner >> shift_of(gy))
    high = placed * per_owner + (high & (per_owner - 1))
    hot_hi[...] = one_hot(high, gx * gy * per_owner)
    hot_lo[...] = one_hot(key & (LANES - 1), LANES)

    for load in loads[:4]:
        load.wait()

    def pack_edges(i, carry):
        for j in range(3):

            def pack(z, carry):
                left, right = carry
                moved = pltpu.roll(coup[0, i, j, z][:, :LANES], z, 1)
                left = jnp.where(lane == z, moved, left)
                moved = pltpu.roll(coup[1, i, j, z][:, cx - LANES :], z + 1, 1)
                right = jnp.where(lane == z, moved, right)
                cy_edge[0, i, j, pl.ds(z, 1), :] = coup[2, i, j, z, 0:1, :]
                cy_edge[1, i, j, pl.ds(z, 1), :] = coup[3, i, j, z, cy - 1 : cy, :]
                return left, right

            left, right = lax.fori_loop(0, nz, pack, no_packs[:2], unroll=16)
            cx_edge[0, i, j] = left
            cx_edge[1, i, j] = right
        return carry

    lax.fori_loop(0, 3, pack_edges, 0)
    for load in loads[4:]:
        load.wait()

    def one_turn(turn, carry):
        colour = 3 - jnp.abs(turn - 3)
        lax.fori_loop(0, nz, interior, 0, unroll=4)
        take_halo(turn - 1)
        packs = sweep_layers(turn, functools.partial(finish, turn, colour))

        @pl.when(turn < 6)
        def _():
            send_halo(turn, packs)

        return carry

    lax.fori_loop(1, 7, one_turn, 0)

    for u in range(3):
        for k, part in enumerate(parts_of(fld[u, 1 : nz + 1].reshape(nz * cy, cx), 2)):
            field_parts[u, k] = part
    chunk = min(perfs, 256)
    row_index = lax.broadcasted_iota(jnp.int32, (nz * cy, chunk), 0)

    def read_terms(c, carry):
        at = pl.ds(pl.multiple_of(c * chunk, chunk), chunk)
        column = hot_x[:, at]
        term = jnp.zeros((nz * cy, chunk), F32)
        for u in range(3):
            read = dot_nn(field_parts[u, 0], column) + dot_nn(field_parts[u, 1], column)
            term = term + read * gather[u : u + 1, at]
        there = cells[:, at] >> shift_of(cx)
        terms[:, at] = jnp.sum(jnp.where(row_index == there, term, 0.0), axis=0, keepdims=True)
        return carry

    lax.fori_loop(0, perfs // chunk, read_terms, 0)
    sums = sum(dot_nt(hot_hi[...], hot_lo[...] * part) for part in parts_of(terms[...]))
    totals[...] = sums.reshape(totals.shape)

    def along_gy(src, dst, send, recv, d):
        return pltpu.make_async_remote_copy(
            src_ref=src,
            dst_ref=dst,
            send_sem=send.at[d],
            recv_sem=recv.at[d],
            device_id=(ix, lax.rem(iy + d, gy)),
            device_id_type=MESH,
        )

    def along_gx(src, dst, send, recv, d):
        return pltpu.make_async_remote_copy(
            src_ref=src,
            dst_ref=dst,
            send_sem=send.at[d],
            recv_sem=recv.at[d],
            device_id=(lax.rem(ix + d, gx), iy),
            device_id_type=MESH,
        )

    copies_a = [
        along_gy(totals.at[lax.rem(iy + d, gy)], got_a.at[d], a_send, a_recv, d)
        for d in range(1, gy)
    ]
    for copy in copies_a:
        copy.start()

    first_well = (ix * gy + iy) * owned
    at_row = lax.div(first_well, LANES)
    at_lane = lax.rem(first_well, LANES)

    def own_row(table):
        line = jnp.broadcast_to(table[pl.ds(at_row, 1), :], (8, LANES))
        return pltpu.roll(line, LANES - at_lane, 1)[0:1, :owned]

    slot_row = own_row(slots) - first_well
    count_row = own_row(counts)
    down = lax.broadcasted_iota(jnp.int32, (owned, owned), 0)
    across = lax.broadcasted_iota(jnp.int32, (owned, owned), 1)
    slot_column = jnp.sum(jnp.where(down == across, slot_row, 0), axis=1, keepdims=True)
    count_column = jnp.sum(jnp.where(down == across, count_row, 0), axis=1, keepdims=True)
    to_slot = jnp.where(slot_row == down, 1.0, 0.0).astype(BF16)
    of_well = slot_column == across
    to_well = jnp.where(of_well, 1.0, 0.0).astype(BF16)
    live = jnp.sum(jnp.where(of_well, count_column, 0), axis=0, keepdims=True)
    alive = lax.broadcasted_iota(jnp.int32, (seg, owned), 0) < live
    wells_row = LANES // seg
    lane_of = lax.broadcasted_iota(jnp.int32, (owned, LANES), 1)
    well_of = lax.broadcasted_iota(jnp.int32, (owned, LANES), 0)
    mine = (lane_of >> shift_of(seg)) == (well_of & (wells_row - 1))
    fold_from = lax.broadcasted_iota(jnp.int32, (seg, LANES), 1)
    fold_to = lax.broadcasted_iota(jnp.int32, (seg, LANES), 0)
    fold = jnp.where((fold_from & (seg - 1)) == fold_to, 1.0, 0.0).astype(BF16)

    for copy in copies_a:
        copy.wait_recv()
    summed = totals[iy]
    for d in range(1, gy):
        summed = summed + got_a[d]
    sum_a[...] = summed
    copies_b = [
        along_gx(sum_a.at[lax.rem(ix + d, gx)], got_b.at[d], b_send, b_recv, d)
        for d in range(1, gx)
    ]
    for copy in copies_b:
        copy.start()
    for copy in copies_b:
        copy.wait_recv()
    own = sum_a[ix]
    for d in range(1, gx):
        own = own + got_b[d]

    rows = jnp.broadcast_to(own[:, None, :], (per_owner, wells_row, LANES)).reshape(owned, LANES)
    by_well = sum(dot_nt(fold, part) for part in parts_of(jnp.where(mine, rows, 0.0)))
    by_slot = sum(dot_nt(part, to_slot) for part in parts_of(by_well))
    by_slot = jnp.where(alive, by_slot, 0.0)
    solved = jnp.sum(inverses[...] * by_slot[None], axis=1)
    solved = jnp.where(alive, solved, 0.0)
    solved = sum(dot_nt(to_well, part) for part in parts_of(solved))
    solved = sum(dot_nn(part, fold) for part in parts_of(solved))
    solved = jnp.where(mine, solved, 0.0)
    values[iy, ix] = jnp.sum(solved.reshape(per_owner, wells_row, LANES), axis=1)

    def sent_c(d):
        return along_gx(values.at[iy, ix], values.at[iy, ix], c_send, c_recv, d)

    def due_c(d):
        there = lax.rem(ix + gx - d, gx)
        return along_gx(values.at[iy, there], values.at[iy, there], c_send, c_recv, d)

    for d in range(1, gx):
        sent_c(d).start()
    for d in range(1, gx):
        due_c(d).wait_recv()

    def sent_d(d):
        return along_gy(values.at[iy], values.at[iy], d_send, d_recv, d)

    def due_d(d):
        there = lax.rem(iy + gy - d, gy)
        return along_gy(values.at[there], values.at[there], d_send, d_recv, d)

    for d in range(1, gy):
        sent_d(d).start()
    for d in range(1, gy):
        due_d(d).wait_recv()

    table = values[...].reshape(gx * gy * per_owner, LANES)
    table_parts = parts_of(table)
    for c in range(perfs // chunk):
        at = pl.ds(c * chunk, chunk)
        column = hot_lo[:, at]
        read = sum(dot_nn(part, column) for part in table_parts)
        terms[:, at] = jnp.sum(read * hot_hi[:, at].astype(F32), axis=0, keepdims=True)
    at_perfs = terms[...]
    for u in range(3):
        weights = parts_of(ret[u : u + 1, :] * at_perfs, 2)
        change = sum(dot_nt(hot_r[...], hot_x[...] * part) for part in weights)
        out[u] = fld[u, 1 : nz + 1] - change.reshape(nz, cy, cx)

    for done in range(6):
        for pair in [x_copies(done)] + [y_copies(done, c) for c in range(nz // depth)]:
            for copy, inside in pair:
                pl.when(inside)(copy.wait_send)
    for copy in copies_a + copies_b:
        copy.wait_send()
    for d in range(1, gx):
        sent_c(d).wait_send()
    for d in range(1, gy):
        sent_d(d).wait_send()


def shards(
    gx,
    gy,
    rhs_field,
    couplings,
    pivot_inverses,
    colours,
    perf_cells,
    perf_wells,
    perf_segments,
    perf_gather,
    perf_return,
    well_slot,
    seg_count,
    well_inverses,
):
    _, nz, cy, cx = rhs_field.shape
    owned, seg, _ = well_inverses.shape
    perfs = perf_cells.shape[0]
    per_owner = owned * seg // LANES
    high = gx * gy * per_owner
    hbm = pl.BlockSpec(memory_space=pltpu.HBM)
    dma = pltpu.SemaphoreType.DMA
    operands = (
        rhs_field,
        couplings,
        pivot_inverses,
        colours,
        perf_cells.reshape(1, perfs),
        perf_wells.reshape(1, perfs),
        perf_segments.reshape(1, perfs),
        perf_gather,
        perf_return,
        well_slot.reshape(-1, LANES),
        seg_count.reshape(-1, LANES),
        jnp.transpose(well_inverses, (1, 2, 0)),
    )
    return pl.pallas_call(
        functools.partial(kernel, gx, gy),
        out_shape=jax.ShapeDtypeStruct(rhs_field.shape, F32),
        in_specs=[hbm] * len(operands),
        out_specs=pl.BlockSpec(memory_space=pltpu.VMEM),
        scratch_shapes=[pltpu.VMEM(x.shape, x.dtype) for x in operands]
        + [
            pltpu.VMEM((3, nz + 2, cy, cx), F32),
            pltpu.VMEM((3, nz, cy, cx), F32),
            pltpu.VMEM((2, 3, 3, cy, LANES), F32),
            pltpu.VMEM((2, 3, 3, nz, cx), F32),
            pltpu.VMEM((2, 3, cy, LANES), F32),
            pltpu.VMEM((2, 3, nz, cx), F32),
            pltpu.VMEM((6, 2, 3, cy, LANES), F32),
            pltpu.VMEM((7, 2, 3, nz, cx), F32),
            pltpu.VMEM((6, 2, 3, cy, LANES), F32),
            pltpu.VMEM((6, 2, 3, nz, cx), F32),
            pltpu.VMEM((cx, perfs), BF16),
            pltpu.VMEM((nz * cy, perfs), BF16),
            pltpu.VMEM((high, perfs), BF16),
            pltpu.VMEM((LANES, perfs), BF16),
            pltpu.VMEM((3, 2, nz * cy, cx), BF16),
            pltpu.VMEM((1, perfs), F32),
            pltpu.VMEM((gy, gx, per_owner, LANES), F32),
            pltpu.VMEM((gy, gx, per_owner, LANES), F32),
            pltpu.VMEM((gx, per_owner, LANES), F32),
            pltpu.VMEM((gx, per_owner, LANES), F32),
            pltpu.VMEM((gy, gx, per_owner, LANES), F32),
            dma((6,)),
            dma((11,)),
            dma((6, 2)),
            dma((6, 2)),
            dma((6, nz // 8, 2)),
            dma((6, nz // 8, 2)),
            dma((gy,)),
            dma((gy,)),
            dma((gx,)),
            dma((gx,)),
            dma((gx,)),
            dma((gx,)),
            dma((gy,)),
            dma((gy,)),
        ],
        compiler_params=pltpu.CompilerParams(
            collective_id=0, has_side_effects=True, vmem_limit_bytes=63 * 2**20 + 2**19
        ),
        name="precondition",
    )(*operands)


def solution(mesh):
    return jax.shard_map(
        functools.partial(shards, mesh.shape["gx"], mesh.shape["gy"]),
        mesh=mesh,
        in_specs=(
            P(None, None, "gy", "gx"),
            P(None, None, None, None, "gy", "gx"),
            P(None, None, None, "gy", "gx"),
            P(None, "gy", "gx"),
            P(("gx", "gy")),
            P(("gx", "gy")),
            P(("gx", "gy")),
            P(None, ("gx", "gy")),
            P(None, ("gx", "gy")),
            P(),
            P(),
            P(("gx", "gy"), None, None),
        ),
        out_specs=P(None, None, "gy", "gx"),
        check_vma=False,
    )
```

```python
import functools

import jax
import jax.numpy as jnp
from jax import lax
from jax.experimental import pallas as pl
from jax.experimental.pallas import tpu as pltpu
from jax.sharding import PartitionSpec as P

MESH = pl.DeviceIdType.MESH
LANES = 128
F32 = jnp.float32
BF16 = jnp.bfloat16


def shift_of(n):
    assert n & (n - 1) == 0
    return n.bit_length() - 1


def parts_of(x, count=3):
    parts = []
    for k in range(count):
        part = x.astype(BF16)
        parts.append(part)
        if k + 1 < count:
            x = x - part.astype(F32)
    return parts


def dot_nn(a, b):
    return lax.dot_general(a, b, (((1,), (0,)), ((), ())), preferred_element_type=F32)


def dot_nt(a, b):
    return lax.dot_general(a, b, (((1,), (1,)), ((), ())), preferred_element_type=F32)


def one_hot(row, count):
    index = lax.broadcasted_iota(jnp.int32, (count, row.shape[1]), 0)
    return jnp.where(index == row, 1.0, 0.0).astype(BF16)


def kernel(
    gx,
    gy,
    rhs,
    couplings,
    pivots_in,
    colours_in,
    cells_in,
    wells_in,
    segs_in,
    gather_in,
    ret_in,
    slots_in,
    counts_in,
    inverses_in,
    out,
    upper,
    coup,
    pivots,
    colours,
    cells,
    wells,
    segs,
    gather,
    ret,
    slots,
    counts,
    inverses,
    fld,
    acc,
    cx_edge,
    cy_edge,
    x_add,
    y_add,
    xsend,
    ysend,
    xhalo,
    yhalo,
    hot_x,
    hot_r,
    hot_hi,
    hot_lo,
    field_parts,
    terms,
    totals,
    got,
    values,
    load_sem,
    small_sem,
    x_send,
    x_recv,
    y_send,
    y_recv,
    a_send,
    a_recv,
    b_send,
    b_recv,
):
    _, nz, cy, cx = rhs.shape
    seg, _, owned = inverses.shape
    perfs = cells.shape[1]
    depth = 8
    ix = lax.axis_index("gx")
    iy = lax.axis_index("gy")
    count = gx * gy
    me = ix * gy + iy

    def peer(d):
        there = lax.rem(me + d, count)
        return lax.div(there, gy), lax.rem(there, gy)

    smalls = [
        pltpu.make_async_copy(src, dst, small_sem.at[k])
        for k, (src, dst) in enumerate(
            (
                (rhs, upper),
                (pivots_in, pivots),
                (colours_in, colours),
                (cells_in, cells),
                (wells_in, wells),
                (segs_in, segs),
                (gather_in, gather),
                (ret_in, ret),
                (slots_in, slots),
                (counts_in, counts),
                (inverses_in, inverses),
            )
        )
    ]
    loads = [
        pltpu.make_async_copy(couplings.at[k], coup.at[k], load_sem.at[k]) for k in range(6)
    ]
    for load in smalls + loads:
        load.start()

    barrier = pltpu.get_barrier_semaphore()

    @pl.when(ix == 0)
    def _():
        xhalo[:, 0] = jnp.zeros_like(xhalo[:, 0])

    @pl.when(ix == gx - 1)
    def _():
        xhalo[:, 1] = jnp.zeros_like(xhalo[:, 1])

    @pl.when(iy == 0)
    def _():
        yhalo[:, 0] = jnp.zeros_like(yhalo[:, 0])

    @pl.when(iy == gy - 1)
    def _():
        yhalo[:, 1] = jnp.zeros_like(yhalo[:, 1])

    def greet(d, carry):
        pl.semaphore_signal(barrier, inc=1, device_id=peer(d), device_id_type=MESH)
        return carry

    lax.fori_loop(1, count, greet, 0)

    lane = lax.broadcasted_iota(jnp.int32, (cy, LANES), 1)
    wide_lane = lax.broadcasted_iota(jnp.int32, (cy, cx), 1)
    row = lax.broadcasted_iota(jnp.int32, (cy, cx), 0)
    tiles = cx // LANES

    for u in range(3):
        fld[u, 0] = jnp.zeros((cy, cx), F32)
        fld[u, nz + 1] = jnp.zeros((cy, cx), F32)

    def pivoted(z, field):
        return [
            pivots[i, 0, z] * field[0] + pivots[i, 1, z] * field[1] + pivots[i, 2, z] * field[2]
            for i in range(3)
        ]

    def emit(slot, z, new, packs):
        result = []
        for j in range(3):
            ysend[slot, 0, j, pl.ds(z, 1), :] = new[j][cy - 1 : cy]
            ysend[slot, 1, j, pl.ds(z, 1), :] = new[j][0:1]
        for j in range(3):
            moved = pltpu.roll(new[j][:, cx - LANES :], z + 1, 1)
            result.append(jnp.where(lane == z, moved, packs[j]))
        for j in range(3):
            moved = pltpu.roll(new[j][:, :LANES], z, 1)
            result.append(jnp.where(lane == z, moved, packs[3 + j]))
        return tuple(result)

    no_packs = tuple(jnp.zeros((cy, LANES), F32) for _ in range(6))

    def x_copies(slot):
        found = []
        for side, there, inside in ((0, ix + 1, ix < gx - 1), (1, ix - 1, ix > 0)):
            copy = pltpu.make_async_remote_copy(
                src_ref=xsend.at[slot, side],
                dst_ref=xhalo.at[slot, side],
                send_sem=x_send.at[slot, side],
                recv_sem=x_recv.at[slot, side],
                device_id=(there, iy),
                device_id_type=MESH,
            )
            found.append((copy, inside))
        return found

    def y_copies(slot, layers):
        found = []
        for side, there, inside in ((0, iy + 1, iy < gy - 1), (1, iy - 1, iy > 0)):
            copy = pltpu.make_async_remote_copy(
                src_ref=ysend.at[slot, side, :, layers, :],
                dst_ref=yhalo.at[slot, side, :, layers, :],
                send_sem=y_send.at[slot, side],
                recv_sem=y_recv.at[slot, side],
                device_id=(ix, there),
                device_id_type=MESH,
            )
            found.append((copy, inside))
        return found

    def sweep_layers(slot, body):
        def some(c, packs):
            for k in range(depth):
                packs = body(c * depth + k, packs)

            @pl.when(slot < 6)
            def _():
                layers = pl.ds(pl.multiple_of(c * depth, depth), depth)
                for copy, inside in y_copies(slot, layers):
                    pl.when(inside)(copy.start)

            return packs

        return lax.fori_loop(0, nz // depth, some, no_packs)

    def send_halo(slot, packs):
        for j in range(3):
            xsend[slot, 0, j] = packs[j]
            xsend[slot, 1, j] = packs[3 + j]
        for copy, inside in x_copies(slot):
            pl.when(inside)(copy.start)

    def take_halo(slot):
        for pair in (x_copies(slot), y_copies(slot, slice(None))):
            pl.when(pair[1][1])(pair[0][0].wait_recv)
            pl.when(pair[0][1])(pair[1][0].wait_recv)
        for side in range(2):
            for i in range(3):
                x_add[side, i] = sum(cx_edge[side, i, j] * xhalo[slot, side, j] for j in range(3))
                y_add[side, i] = sum(cy_edge[side, i, j] * yhalo[slot, side, j] for j in range(3))

    def interior(z, carry):
        total = [upper[i, z] for i in range(3)]
        for j in range(3):
            here = fld[j, z + 1]
            beside = (
                jnp.where(wide_lane == 0, 0.0, pltpu.roll(here, 1, 1)),
                jnp.where(wide_lane == cx - 1, 0.0, pltpu.roll(here, cx - 1, 1)),
                jnp.where(row == 0, 0.0, pltpu.roll(here, 1, 0)),
                jnp.where(row == cy - 1, 0.0, pltpu.roll(here, cy - 1, 0)),
                fld[j, z],
                fld[j, z + 2],
            )
            for i in range(3):
                for k in range(6):
                    total[i] = total[i] - coup[k, i, j, z] * beside[k]
        for i in range(3):
            acc[i, z] = total[i]
        return carry

    def finish(turn, colour, z, packs):
        current = []
        for i in range(3):
            first = jnp.where(lane == 0, pltpu.roll(x_add[0, i], LANES - z, 1), 0.0)
            last = jnp.where(lane == LANES - 1, pltpu.roll(x_add[1, i], LANES - 1 - z, 1), 0.0)
            pieces = [jnp.zeros((cy, LANES), F32)] * tiles
            pieces[0] = pieces[0] + first
            pieces[-1] = pieces[-1] + last
            along_x = jnp.concatenate(pieces, axis=1) if tiles > 1 else pieces[0]
            along_y = jnp.where(row == 0, y_add[0, i, pl.ds(z, 1), :], 0.0) + jnp.where(
                row == cy - 1, y_add[1, i, pl.ds(z, 1), :], 0.0
            )
            current.append(acc[i, z] - along_x - along_y)
        chosen = colours[z] == colour
        new = pivoted(z, current)
        kept = jnp.where(turn == 3, 0.0, 1.0)
        for i in range(3):
            upper[i, z] = jnp.where(chosen, current[i], upper[i, z])
            new[i] = jnp.where(chosen, new[i], fld[i, z + 1] * kept)
            fld[i, z + 1] = new[i]
        return emit(turn, z, new, packs)

    def first(z, packs):
        chosen = colours[z] == 0
        new = pivoted(z, [upper[i, z] for i in range(3)])
        for i in range(3):
            new[i] = jnp.where(chosen, new[i], 0.0)
            fld[i, z + 1] = new[i]
        return emit(0, z, new, packs)

    for load in smalls[:3]:
        load.wait()
    pl.semaphore_wait(barrier, count - 1)
    packs = sweep_layers(0, first)
    send_halo(0, packs)

    for load in smalls[3:]:
        load.wait()
    cell = cells[...]
    key = wells[...] * seg + segs[...]
    hot_x[...] = one_hot(cell & (cx - 1), cx)
    hot_r[...] = one_hot(cell >> shift_of(cx), nz * cy)
    per_owner = owned * seg // LANES
    high = key >> shift_of(LANES)
    owner = high >> shift_of(per_owner)
    offset = (owner - me) & (count - 1)
    high = offset * per_owner + (high & (per_owner - 1))
    hot_hi[...] = one_hot(high, count * per_owner)
    hot_lo[...] = one_hot(key & (LANES - 1), LANES)

    for load in loads[:4]:
        load.wait()

    def pack_edges(i, carry):
        for j in range(3):

            def pack(z, carry):
                left, right = carry
                moved = pltpu.roll(coup[0, i, j, z][:, :LANES], z, 1)
                left = jnp.where(lane == z, moved, left)
                moved = pltpu.roll(coup[1, i, j, z][:, cx - LANES :], z + 1, 1)
                right = jnp.where(lane == z, moved, right)
                cy_edge[0, i, j, pl.ds(z, 1), :] = coup[2, i, j, z, 0:1, :]
                cy_edge[1, i, j, pl.ds(z, 1), :] = coup[3, i, j, z, cy - 1 : cy, :]
                return left, right

            left, right = lax.fori_loop(0, nz, pack, no_packs[:2], unroll=16)
            cx_edge[0, i, j] = left
            cx_edge[1, i, j] = right
        return carry

    lax.fori_loop(0, 3, pack_edges, 0)
    for load in loads[4:]:
        load.wait()

    def one_turn(turn, carry):
        colour = 3 - jnp.abs(turn - 3)
        lax.fori_loop(0, nz, interior, 0, unroll=4)
        take_halo(turn - 1)
        packs = sweep_layers(turn, functools.partial(finish, turn, colour))

        @pl.when(turn < 6)
        def _():
            send_halo(turn, packs)

        return carry

    lax.fori_loop(1, 7, one_turn, 0)

    for u in range(3):
        for k, part in enumerate(parts_of(fld[u, 1 : nz + 1].reshape(nz * cy, cx), 2)):
            field_parts[u, k] = part
    chunk = min(perfs, 256)
    row_index = lax.broadcasted_iota(jnp.int32, (nz * cy, chunk), 0)

    def read_terms(c, carry):
        at = pl.ds(pl.multiple_of(c * chunk, chunk), chunk)
        column = hot_x[:, at]
        term = jnp.zeros((nz * cy, chunk), F32)
        for u in range(3):
            read = dot_nn(field_parts[u, 0], column) + dot_nn(field_parts[u, 1], column)
            term = term + read * gather[u : u + 1, at]
        there = cells[:, at] >> shift_of(cx)
        terms[:, at] = jnp.sum(jnp.where(row_index == there, term, 0.0), axis=0, keepdims=True)
        return carry

    lax.fori_loop(0, perfs // chunk, read_terms, 0)
    sums = sum(dot_nt(hot_hi[...], hot_lo[...] * part) for part in parts_of(terms[...]))
    totals[...] = sums.reshape(totals.shape)

    def sent_totals(d, blocks=1):
        return pltpu.make_async_remote_copy(
            src_ref=totals.at[pl.ds(d, blocks)],
            dst_ref=got.at[pl.ds(d, blocks)],
            send_sem=a_send,
            recv_sem=a_recv,
            device_id=peer(d),
            device_id_type=MESH,
        )

    def start_totals(d, carry):
        sent_totals(d).start()
        return carry

    lax.fori_loop(1, count, start_totals, 0)

    first_well = me * owned
    at_row = lax.div(first_well, LANES)
    at_lane = lax.rem(first_well, LANES)

    def own_row(table):
        line = jnp.broadcast_to(table[pl.ds(at_row, 1), :], (8, LANES))
        return pltpu.roll(line, LANES - at_lane, 1)[0:1, :owned]

    slot_row = own_row(slots) - first_well
    count_row = own_row(counts)
    down = lax.broadcasted_iota(jnp.int32, (owned, owned), 0)
    across = lax.broadcasted_iota(jnp.int32, (owned, owned), 1)
    slot_column = jnp.sum(jnp.where(down == across, slot_row, 0), axis=1, keepdims=True)
    count_column = jnp.sum(jnp.where(down == across, count_row, 0), axis=1, keepdims=True)
    to_slot = jnp.where(slot_row == down, 1.0, 0.0).astype(BF16)
    of_well = slot_column == across
    to_well = jnp.where(of_well, 1.0, 0.0).astype(BF16)
    live = jnp.sum(jnp.where(of_well, count_column, 0), axis=0, keepdims=True)
    alive = lax.broadcasted_iota(jnp.int32, (seg, owned), 0) < live
    wells_row = LANES // seg
    lane_of = lax.broadcasted_iota(jnp.int32, (owned, LANES), 1)
    well_of = lax.broadcasted_iota(jnp.int32, (owned, LANES), 0)
    mine = (lane_of >> shift_of(seg)) == (well_of & (wells_row - 1))
    fold_from = lax.broadcasted_iota(jnp.int32, (seg, LANES), 1)
    fold_to = lax.broadcasted_iota(jnp.int32, (seg, LANES), 0)
    fold = jnp.where((fold_from & (seg - 1)) == fold_to, 1.0, 0.0).astype(BF16)

    sent_totals(1, count - 1).wait_recv()
    own = totals[0] + jnp.sum(got[1:], axis=0)

    rows = jnp.broadcast_to(own[:, None, :], (per_owner, wells_row, LANES)).reshape(owned, LANES)
    by_well = sum(dot_nt(fold, part) for part in parts_of(jnp.where(mine, rows, 0.0)))
    by_slot = sum(dot_nt(part, to_slot) for part in parts_of(by_well))
    by_slot = jnp.where(alive, by_slot, 0.0)
    solved = jnp.sum(inverses[...] * by_slot[None], axis=1)
    solved = jnp.where(alive, solved, 0.0)
    solved = sum(dot_nt(to_well, part) for part in parts_of(solved))
    solved = sum(dot_nn(part, fold) for part in parts_of(solved))
    solved = jnp.where(mine, solved, 0.0)
    values[0] = jnp.sum(solved.reshape(per_owner, wells_row, LANES), axis=1)

    def sent_values(d):
        return pltpu.make_async_remote_copy(
            src_ref=values.at[pl.ds(0, 1)],
            dst_ref=values.at[pl.ds(count - d, 1)],
            send_sem=b_send,
            recv_sem=b_recv,
            device_id=peer(d),
            device_id_type=MESH,
        )

    def start_values(d, carry):
        sent_values(d).start()
        return carry

    lax.fori_loop(1, count, start_values, 0)
    others = values.at[pl.ds(1, count - 1)]
    all_values = pltpu.make_async_remote_copy(
        src_ref=others,
        dst_ref=others,
        send_sem=b_send,
        recv_sem=b_recv,
        device_id=peer(1),
        device_id_type=MESH,
    )
    all_values.wait_recv()

    table = values[...].reshape(count * per_owner, LANES)
    table_parts = parts_of(table)
    for c in range(perfs // chunk):
        at = pl.ds(c * chunk, chunk)
        column = hot_lo[:, at]
        read = sum(dot_nn(part, column) for part in table_parts)
        terms[:, at] = jnp.sum(read * hot_hi[:, at].astype(F32), axis=0, keepdims=True)
    at_perfs = terms[...]
    for u in range(3):
        weights = parts_of(ret[u : u + 1, :] * at_perfs, 2)
        change = sum(dot_nt(hot_r[...], hot_x[...] * part) for part in weights)
        out[u] = fld[u, 1 : nz + 1] - change.reshape(nz, cy, cx)

    for done in range(6):
        for pair in (x_copies(done), y_copies(done, slice(None))):
            for copy, inside in pair:
                pl.when(inside)(copy.wait_send)
    sent_totals(1, count - 1).wait_send()
    all_values.wait_send()


def shards(
    gx,
    gy,
    rhs_field,
    couplings,
    pivot_inverses,
    colours,
    perf_cells,
    perf_wells,
    perf_segments,
    perf_gather,
    perf_return,
    well_slot,
    seg_count,
    well_inverses,
):
    _, nz, cy, cx = rhs_field.shape
    owned, seg, _ = well_inverses.shape
    perfs = perf_cells.shape[0]
    per_owner = owned * seg // LANES
    high = gx * gy * per_owner
    hbm = pl.BlockSpec(memory_space=pltpu.HBM)
    dma = pltpu.SemaphoreType.DMA
    operands = (
        rhs_field,
        couplings,
        pivot_inverses,
        colours,
        perf_cells.reshape(1, perfs),
        perf_wells.reshape(1, perfs),
        perf_segments.reshape(1, perfs),
        perf_gather,
        perf_return,
        well_slot.reshape(-1, LANES),
        seg_count.reshape(-1, LANES),
        jnp.transpose(well_inverses, (1, 2, 0)),
    )
    return pl.pallas_call(
        functools.partial(kernel, gx, gy),
        out_shape=jax.ShapeDtypeStruct(rhs_field.shape, F32),
        in_specs=[hbm] * len(operands),
        out_specs=pl.BlockSpec(memory_space=pltpu.VMEM),
        scratch_shapes=[pltpu.VMEM(x.shape, x.dtype) for x in operands]
        + [
            pltpu.VMEM((3, nz + 2, cy, cx), F32),
            pltpu.VMEM((3, nz, cy, cx), F32),
            pltpu.VMEM((2, 3, 3, cy, LANES), F32),
            pltpu.VMEM((2, 3, 3, nz, cx), F32),
            pltpu.VMEM((2, 3, cy, LANES), F32),
            pltpu.VMEM((2, 3, nz, cx), F32),
            pltpu.VMEM((6, 2, 3, cy, LANES), F32),
            pltpu.VMEM((7, 2, 3, nz, cx), F32),
            pltpu.VMEM((6, 2, 3, cy, LANES), F32),
            pltpu.VMEM((6, 2, 3, nz, cx), F32),
            pltpu.VMEM((cx, perfs), BF16),
            pltpu.VMEM((nz * cy, perfs), BF16),
            pltpu.VMEM((high, perfs), BF16),
            pltpu.VMEM((LANES, perfs), BF16),
            pltpu.VMEM((3, 2, nz * cy, cx), BF16),
            pltpu.VMEM((1, perfs), F32),
            pltpu.VMEM((gx * gy, per_owner, LANES), F32),
            pltpu.VMEM((gx * gy, per_owner, LANES), F32),
            pltpu.VMEM((gx * gy, per_owner, LANES), F32),
            dma((6,)),
            dma((11,)),
            dma((6, 2)),
            dma((6, 2)),
            dma((6, 2)),
            dma((6, 2)),
            dma,
            dma,
            dma,
            dma,
        ],
        compiler_params=pltpu.CompilerParams(
            collective_id=0, has_side_effects=True, vmem_limit_bytes=63 * 2**20 + 2**19
        ),
        name="precondition",
    )(*operands)


def solution(mesh):
    return jax.shard_map(
        functools.partial(shards, mesh.shape["gx"], mesh.shape["gy"]),
        mesh=mesh,
        in_specs=(
            P(None, None, "gy", "gx"),
            P(None, None, None, None, "gy", "gx"),
            P(None, None, None, "gy", "gx"),
            P(None, "gy", "gx"),
            P(("gx", "gy")),
            P(("gx", "gy")),
            P(("gx", "gy")),
            P(None, ("gx", "gy")),
            P(None, ("gx", "gy")),
            P(),
            P(),
            P(("gx", "gy"), None, None),
        ),
        out_specs=P(None, None, "gy", "gx"),
        check_vma=False,
    )
```

```python
import functools

import jax
import jax.numpy as jnp
from jax import lax
from jax.experimental import pallas as pl
from jax.experimental.pallas import tpu as pltpu
from jax.sharding import PartitionSpec as P

MESH = pl.DeviceIdType.MESH
LANES = 128
F32 = jnp.float32
BF16 = jnp.bfloat16


def shift_of(n):
    assert n & (n - 1) == 0
    return n.bit_length() - 1


def parts_of(x, count=3):
    parts = []
    for k in range(count):
        part = x.astype(BF16)
        parts.append(part)
        if k + 1 < count:
            x = x - part.astype(F32)
    return parts


def dot_nn(a, b):
    return lax.dot_general(a, b, (((1,), (0,)), ((), ())), preferred_element_type=F32)


def dot_nt(a, b):
    return lax.dot_general(a, b, (((1,), (1,)), ((), ())), preferred_element_type=F32)


def one_hot(row, count):
    index = lax.broadcasted_iota(jnp.int32, (count, row.shape[1]), 0)
    return jnp.where(index == row, 1.0, 0.0).astype(BF16)


def kernel(
    gx,
    gy,
    rhs,
    couplings,
    pivots_in,
    colours_in,
    cells_in,
    wells_in,
    segs_in,
    gather_in,
    ret_in,
    slots_in,
    counts_in,
    inverses_in,
    out,
    upper,
    coup,
    pivots,
    colours,
    cells,
    wells,
    segs,
    gather,
    ret,
    slots,
    counts,
    inverses,
    fld,
    acc,
    cx_edge,
    cy_edge,
    x_add,
    y_add,
    xsend,
    ysend,
    xhalo,
    yhalo,
    hot_x,
    hot_r,
    hot_hi,
    hot_lo,
    field_parts,
    terms,
    totals,
    got,
    values,
    load_sem,
    small_sem,
    store_sem,
    x_send,
    x_recv,
    y_send,
    y_recv,
    a_send,
    a_recv,
    b_send,
    b_recv,
):
    _, nz, cy, cx = rhs.shape
    seg, _, owned = inverses.shape
    perfs = cells.shape[1]
    depth = 8
    ix = lax.axis_index("gx")
    iy = lax.axis_index("gy")
    count = gx * gy
    me = ix * gy + iy

    def peer(d):
        there = lax.rem(me + d, count)
        return lax.div(there, gy), lax.rem(there, gy)

    smalls = [
        pltpu.make_async_copy(src, dst, small_sem.at[k])
        for k, (src, dst) in enumerate(
            (
                (rhs, upper),
                (pivots_in, pivots),
                (colours_in, colours),
                (cells_in, cells),
                (wells_in, wells),
                (segs_in, segs),
                (gather_in, gather),
                (ret_in, ret),
                (slots_in, slots),
                (counts_in, counts),
                (inverses_in, inverses),
            )
        )
    ]
    loads = [
        pltpu.make_async_copy(couplings.at[k], coup.at[k], load_sem.at[k]) for k in range(6)
    ]
    for load in smalls + loads:
        load.start()

    barrier = pltpu.get_barrier_semaphore()

    @pl.when(ix == 0)
    def _():
        xhalo[:, 0] = jnp.zeros_like(xhalo[:, 0])

    @pl.when(ix == gx - 1)
    def _():
        xhalo[:, 1] = jnp.zeros_like(xhalo[:, 1])

    @pl.when(iy == 0)
    def _():
        yhalo[:, 0] = jnp.zeros_like(yhalo[:, 0])

    @pl.when(iy == gy - 1)
    def _():
        yhalo[:, 1] = jnp.zeros_like(yhalo[:, 1])

    def greet(d, carry):
        pl.semaphore_signal(barrier, inc=1, device_id=peer(d), device_id_type=MESH)
        return carry

    lax.fori_loop(1, count, greet, 0)

    lane = lax.broadcasted_iota(jnp.int32, (cy, LANES), 1)
    wide_lane = lax.broadcasted_iota(jnp.int32, (cy, cx), 1)
    row = lax.broadcasted_iota(jnp.int32, (cy, cx), 0)
    tiles = cx // LANES

    for u in range(3):
        fld[u, 0] = jnp.zeros((cy, cx), F32)
        fld[u, nz + 1] = jnp.zeros((cy, cx), F32)

    def pivoted(z, field):
        return [
            pivots[i, 0, z] * field[0] + pivots[i, 1, z] * field[1] + pivots[i, 2, z] * field[2]
            for i in range(3)
        ]

    def emit(slot, z, new, packs):
        result = []
        for j in range(3):
            ysend[slot, 0, j, pl.ds(z, 1), :] = new[j][cy - 1 : cy]
            ysend[slot, 1, j, pl.ds(z, 1), :] = new[j][0:1]
        for j in range(3):
            moved = pltpu.roll(new[j][:, cx - LANES :], z + 1, 1)
            result.append(jnp.where(lane == z, moved, packs[j]))
        for j in range(3):
            moved = pltpu.roll(new[j][:, :LANES], z, 1)
            result.append(jnp.where(lane == z, moved, packs[3 + j]))
        return tuple(result)

    no_packs = tuple(jnp.zeros((cy, LANES), F32) for _ in range(6))

    def x_copies(slot):
        found = []
        for side, there, inside in ((0, ix + 1, ix < gx - 1), (1, ix - 1, ix > 0)):
            copy = pltpu.make_async_remote_copy(
                src_ref=xsend.at[slot, side],
                dst_ref=xhalo.at[slot, side],
                send_sem=x_send.at[slot, side],
                recv_sem=x_recv.at[slot, side],
                device_id=(there, iy),
                device_id_type=MESH,
            )
            found.append((copy, inside))
        return found

    def y_copies(slot, layers):
        found = []
        for side, there, inside in ((0, iy + 1, iy < gy - 1), (1, iy - 1, iy > 0)):
            copy = pltpu.make_async_remote_copy(
                src_ref=ysend.at[slot, side, :, layers, :],
                dst_ref=yhalo.at[slot, side, :, layers, :],
                send_sem=y_send.at[slot, side],
                recv_sem=y_recv.at[slot, side],
                device_id=(ix, there),
                device_id_type=MESH,
            )
            found.append((copy, inside))
        return found

    def sweep_layers(slot, body):
        def some(c, packs):
            for k in range(depth):
                packs = body(c * depth + k, packs)

            @pl.when(slot < 6)
            def _():
                layers = pl.ds(pl.multiple_of(c * depth, depth), depth)
                for copy, inside in y_copies(slot, layers):
                    pl.when(inside)(copy.start)

            return packs

        return lax.fori_loop(0, nz // depth, some, no_packs)

    def send_halo(slot, packs):
        for j in range(3):
            xsend[slot, 0, j] = packs[j]
            xsend[slot, 1, j] = packs[3 + j]
        for copy, inside in x_copies(slot):
            pl.when(inside)(copy.start)

    def take_halo(slot):
        for pair in (x_copies(slot), y_copies(slot, slice(None))):
            pl.when(pair[1][1])(pair[0][0].wait_recv)
            pl.when(pair[0][1])(pair[1][0].wait_recv)
        for side in range(2):
            for i in range(3):
                x_add[side, i] = sum(cx_edge[side, i, j] * xhalo[slot, side, j] for j in range(3))
                y_add[side, i] = sum(cy_edge[side, i, j] * yhalo[slot, side, j] for j in range(3))

    def interior(z, carry):
        here = [fld[j, z + 1] for j in range(3)]
        shifted = []
        for j in range(3):
            shifted += [
                (2, j, jnp.where(row == 0, 0.0, pltpu.roll(here[j], 1, 0))),
                (3, j, jnp.where(row == cy - 1, 0.0, pltpu.roll(here[j], cy - 1, 0))),
                (0, j, jnp.where(wide_lane == 0, 0.0, pltpu.roll(here[j], 1, 1))),
                (1, j, jnp.where(wide_lane == cx - 1, 0.0, pltpu.roll(here[j], cx - 1, 1))),
            ]
        total = [upper[i, z] for i in range(3)]
        for j in range(3):
            below, above = fld[j, z], fld[j, z + 2]
            for i in range(3):
                total[i] = total[i] - coup[4, i, j, z] * below
                total[i] = total[i] - coup[5, i, j, z] * above
        for i in range(3):
            across = sum(coup[k, i, j, z] * beside for k, j, beside in shifted)
            acc[i, z] = total[i] - across
        return carry

    def finish(turn, colour, z, packs):
        current = []
        for i in range(3):
            first = jnp.where(lane == 0, pltpu.roll(x_add[0, i], LANES - z, 1), 0.0)
            last = jnp.where(lane == LANES - 1, pltpu.roll(x_add[1, i], LANES - 1 - z, 1), 0.0)
            pieces = [jnp.zeros((cy, LANES), F32)] * tiles
            pieces[0] = pieces[0] + first
            pieces[-1] = pieces[-1] + last
            along_x = jnp.concatenate(pieces, axis=1) if tiles > 1 else pieces[0]
            along_y = jnp.where(row == 0, y_add[0, i, pl.ds(z, 1), :], 0.0) + jnp.where(
                row == cy - 1, y_add[1, i, pl.ds(z, 1), :], 0.0
            )
            current.append(acc[i, z] - along_x - along_y)
        chosen = colours[z] == colour
        new = pivoted(z, current)
        kept = jnp.where(turn == 3, 0.0, 1.0)
        for i in range(3):
            upper[i, z] = jnp.where(chosen, current[i], upper[i, z])
            new[i] = jnp.where(chosen, new[i], fld[i, z + 1] * kept)
            fld[i, z + 1] = new[i]
        return emit(turn, z, new, packs)

    def first(z, packs):
        chosen = colours[z] == 0
        new = pivoted(z, [upper[i, z] for i in range(3)])
        for i in range(3):
            new[i] = jnp.where(chosen, new[i], 0.0)
            fld[i, z + 1] = new[i]
        return emit(0, z, new, packs)

    for load in smalls[:3]:
        load.wait()
    pl.semaphore_wait(barrier, count - 1)
    packs = sweep_layers(0, first)
    send_halo(0, packs)

    for load in smalls[3:]:
        load.wait()
    cell = cells[...]
    key = wells[...] * seg + segs[...]
    hot_x[...] = one_hot(cell & (cx - 1), cx)
    hot_r[...] = one_hot(cell >> shift_of(cx), nz * cy)
    per_owner = owned * seg // LANES
    high = key >> shift_of(LANES)
    owner = high >> shift_of(per_owner)
    offset = (owner - me) & (count - 1)
    high = offset * per_owner + (high & (per_owner - 1))
    hot_hi[...] = one_hot(high, count * per_owner)
    hot_lo[...] = one_hot(key & (LANES - 1), LANES)

    for load in loads[:4]:
        load.wait()

    def pack_edges(i, carry):
        for j in range(3):

            def pack(z, carry):
                left, right = carry
                moved = pltpu.roll(coup[0, i, j, z][:, :LANES], z, 1)
                left = jnp.where(lane == z, moved, left)
                moved = pltpu.roll(coup[1, i, j, z][:, cx - LANES :], z + 1, 1)
                right = jnp.where(lane == z, moved, right)
                cy_edge[0, i, j, pl.ds(z, 1), :] = coup[2, i, j, z, 0:1, :]
                cy_edge[1, i, j, pl.ds(z, 1), :] = coup[3, i, j, z, cy - 1 : cy, :]
                return left, right

            left, right = lax.fori_loop(0, nz, pack, no_packs[:2], unroll=16)
            cx_edge[0, i, j] = left
            cx_edge[1, i, j] = right
        return carry

    lax.fori_loop(0, 3, pack_edges, 0)
    for load in loads[4:]:
        load.wait()

    def one_turn(turn, carry):
        colour = 3 - jnp.abs(turn - 3)
        lax.fori_loop(0, nz, interior, 0, unroll=8)
        take_halo(turn - 1)
        packs = sweep_layers(turn, functools.partial(finish, turn, colour))

        @pl.when(turn < 6)
        def _():
            send_halo(turn, packs)

        return carry

    lax.fori_loop(1, 7, one_turn, 0)

    for u in range(3):
        for k, part in enumerate(parts_of(fld[u, 1 : nz + 1].reshape(nz * cy, cx), 2)):
            field_parts[u, k] = part
    chunk = min(perfs, 256)
    row_index = lax.broadcasted_iota(jnp.int32, (nz * cy, chunk), 0)

    def read_terms(c, carry):
        at = pl.ds(pl.multiple_of(c * chunk, chunk), chunk)
        column = hot_x[:, at]
        term = jnp.zeros((nz * cy, chunk), F32)
        for u in range(3):
            read = dot_nn(field_parts[u, 0], column) + dot_nn(field_parts[u, 1], column)
            term = term + read * gather[u : u + 1, at]
        there = cells[:, at] >> shift_of(cx)
        terms[:, at] = jnp.sum(jnp.where(row_index == there, term, 0.0), axis=0, keepdims=True)
        return carry

    lax.fori_loop(0, perfs // chunk, read_terms, 0, unroll=2)
    sums = sum(dot_nt(hot_hi[...], hot_lo[...] * part) for part in parts_of(terms[...]))
    totals[...] = sums.reshape(totals.shape)

    def sent_totals(d, blocks=1):
        return pltpu.make_async_remote_copy(
            src_ref=totals.at[pl.ds(d, blocks)],
            dst_ref=got.at[pl.ds(d, blocks)],
            send_sem=a_send,
            recv_sem=a_recv,
            device_id=peer(d),
            device_id_type=MESH,
        )

    def start_totals(d, carry):
        sent_totals(d).start()
        return carry

    lax.fori_loop(1, count, start_totals, 0)

    first_well = me * owned
    at_row = lax.div(first_well, LANES)
    at_lane = lax.rem(first_well, LANES)

    def own_row(table):
        line = jnp.broadcast_to(table[pl.ds(at_row, 1), :], (8, LANES))
        return pltpu.roll(line, LANES - at_lane, 1)[0:1, :owned]

    slot_row = own_row(slots) - first_well
    count_row = own_row(counts)
    down = lax.broadcasted_iota(jnp.int32, (owned, owned), 0)
    across = lax.broadcasted_iota(jnp.int32, (owned, owned), 1)
    slot_column = jnp.sum(jnp.where(down == across, slot_row, 0), axis=1, keepdims=True)
    count_column = jnp.sum(jnp.where(down == across, count_row, 0), axis=1, keepdims=True)
    to_slot = jnp.where(slot_row == down, 1.0, 0.0).astype(BF16)
    of_well = slot_column == across
    to_well = jnp.where(of_well, 1.0, 0.0).astype(BF16)
    live = jnp.sum(jnp.where(of_well, count_column, 0), axis=0, keepdims=True)
    alive = lax.broadcasted_iota(jnp.int32, (seg, owned), 0) < live
    wells_row = LANES // seg
    lane_of = lax.broadcasted_iota(jnp.int32, (owned, LANES), 1)
    well_of = lax.broadcasted_iota(jnp.int32, (owned, LANES), 0)
    mine = (lane_of >> shift_of(seg)) == (well_of & (wells_row - 1))
    fold_from = lax.broadcasted_iota(jnp.int32, (seg, LANES), 1)
    fold_to = lax.broadcasted_iota(jnp.int32, (seg, LANES), 0)
    fold = jnp.where((fold_from & (seg - 1)) == fold_to, 1.0, 0.0).astype(BF16)

    sent_totals(1, count - 1).wait_recv()
    own = totals[0] + jnp.sum(got[1:], axis=0)

    rows = jnp.broadcast_to(own[:, None, :], (per_owner, wells_row, LANES)).reshape(owned, LANES)
    by_well = sum(dot_nt(fold, part) for part in parts_of(jnp.where(mine, rows, 0.0)))
    by_slot = sum(dot_nt(part, to_slot) for part in parts_of(by_well))
    by_slot = jnp.where(alive, by_slot, 0.0)
    solved = jnp.sum(inverses[...] * by_slot[None], axis=1)
    solved = jnp.where(alive, solved, 0.0)
    solved = sum(dot_nt(to_well, part) for part in parts_of(solved))
    solved = sum(dot_nn(part, fold) for part in parts_of(solved))
    solved = jnp.where(mine, solved, 0.0)
    values[0] = jnp.sum(solved.reshape(per_owner, wells_row, LANES), axis=1)

    def sent_values(d):
        return pltpu.make_async_remote_copy(
            src_ref=values.at[pl.ds(0, 1)],
            dst_ref=values.at[pl.ds(count - d, 1)],
            send_sem=b_send,
            recv_sem=b_recv,
            device_id=peer(d),
            device_id_type=MESH,
        )

    def start_values(d, carry):
        sent_values(d).start()
        return carry

    lax.fori_loop(1, count, start_values, 0)
    others = values.at[pl.ds(1, count - 1)]
    all_values = pltpu.make_async_remote_copy(
        src_ref=others,
        dst_ref=others,
        send_sem=b_send,
        recv_sem=b_recv,
        device_id=peer(1),
        device_id_type=MESH,
    )
    all_values.wait_recv()

    table = values[...].reshape(count * per_owner, LANES)
    table_parts = parts_of(table)
    for c in range(perfs // chunk):
        at = pl.ds(c * chunk, chunk)
        column = hot_lo[:, at]
        read = sum(dot_nn(part, column) for part in table_parts)
        terms[:, at] = jnp.sum(read * hot_hi[:, at].astype(F32), axis=0, keepdims=True)
    at_perfs = terms[...]
    stores = [pltpu.make_async_copy(acc.at[u], out.at[u], store_sem.at[u]) for u in range(3)]
    for u in range(3):
        weights = parts_of(ret[u : u + 1, :] * at_perfs, 2)
        change = sum(dot_nt(hot_r[...], hot_x[...] * part) for part in weights)
        acc[u] = fld[u, 1 : nz + 1] - change.reshape(nz, cy, cx)
        stores[u].start()

    for done in range(6):
        for pair in (x_copies(done), y_copies(done, slice(None))):
            for copy, inside in pair:
                pl.when(inside)(copy.wait_send)
    sent_totals(1, count - 1).wait_send()
    all_values.wait_send()
    for store in stores:
        store.wait()


def shards(
    gx,
    gy,
    rhs_field,
    couplings,
    pivot_inverses,
    colours,
    perf_cells,
    perf_wells,
    perf_segments,
    perf_gather,
    perf_return,
    well_slot,
    seg_count,
    well_inverses,
):
    _, nz, cy, cx = rhs_field.shape
    owned, seg, _ = well_inverses.shape
    perfs = perf_cells.shape[0]
    per_owner = owned * seg // LANES
    high = gx * gy * per_owner
    hbm = pl.BlockSpec(memory_space=pltpu.HBM)
    dma = pltpu.SemaphoreType.DMA
    operands = (
        rhs_field,
        couplings,
        pivot_inverses,
        colours,
        perf_cells.reshape(1, perfs),
        perf_wells.reshape(1, perfs),
        perf_segments.reshape(1, perfs),
        perf_gather,
        perf_return,
        well_slot.reshape(-1, LANES),
        seg_count.reshape(-1, LANES),
        jnp.transpose(well_inverses, (1, 2, 0)),
    )
    return pl.pallas_call(
        functools.partial(kernel, gx, gy),
        out_shape=jax.ShapeDtypeStruct(rhs_field.shape, F32),
        in_specs=[hbm] * len(operands),
        out_specs=hbm,
        scratch_shapes=[pltpu.VMEM(x.shape, x.dtype) for x in operands]
        + [
            pltpu.VMEM((3, nz + 2, cy, cx), F32),
            pltpu.VMEM((3, nz, cy, cx), F32),
            pltpu.VMEM((2, 3, 3, cy, LANES), F32),
            pltpu.VMEM((2, 3, 3, nz, cx), F32),
            pltpu.VMEM((2, 3, cy, LANES), F32),
            pltpu.VMEM((2, 3, nz, cx), F32),
            pltpu.VMEM((6, 2, 3, cy, LANES), F32),
            pltpu.VMEM((7, 2, 3, nz, cx), F32),
            pltpu.VMEM((6, 2, 3, cy, LANES), F32),
            pltpu.VMEM((6, 2, 3, nz, cx), F32),
            pltpu.VMEM((cx, perfs), BF16),
            pltpu.VMEM((nz * cy, perfs), BF16),
            pltpu.VMEM((high, perfs), BF16),
            pltpu.VMEM((LANES, perfs), BF16),
            pltpu.VMEM((3, 2, nz * cy, cx), BF16),
            pltpu.VMEM((1, perfs), F32),
            pltpu.VMEM((gx * gy, per_owner, LANES), F32),
            pltpu.VMEM((gx * gy, per_owner, LANES), F32),
            pltpu.VMEM((gx * gy, per_owner, LANES), F32),
            dma((6,)),
            dma((11,)),
            dma((3,)),
            dma((6, 2)),
            dma((6, 2)),
            dma((6, 2)),
            dma((6, 2)),
            dma,
            dma,
            dma,
            dma,
        ],
        compiler_params=pltpu.CompilerParams(
            collective_id=0, has_side_effects=True, vmem_limit_bytes=63 * 2**20 + 2**19
        ),
        name="precondition",
    )(*operands)


def solution(mesh):
    return jax.shard_map(
        functools.partial(shards, mesh.shape["gx"], mesh.shape["gy"]),
        mesh=mesh,
        in_specs=(
            P(None, None, "gy", "gx"),
            P(None, None, None, None, "gy", "gx"),
            P(None, None, None, "gy", "gx"),
            P(None, "gy", "gx"),
            P(("gx", "gy")),
            P(("gx", "gy")),
            P(("gx", "gy")),
            P(None, ("gx", "gy")),
            P(None, ("gx", "gy")),
            P(),
            P(),
            P(("gx", "gy"), None, None),
        ),
        out_specs=P(None, None, "gy", "gx"),
        check_vma=False,
    )
```
